32 devices in a mesh: dp: 4 (over z), mp: 2 (over core), section: 4 (over y, x).
Axes of the slice: x: 2, y: 2, z: 4, core: 2. Of those that a mesh axis runs over, the one named last changes fastest.
Arguments:
- states: bfloat16 [4096, 8192], P(('dp', 'section'), 'mp'), may hold values from -6 to 6
- direction: bfloat16 [4096, 256], P(('dp', 'section'), 'mp'), may hold values from -0.1875 to 0.1875
- old_logp: bfloat16 [4096], P(('dp', 'section')), may hold values from -4 to -0.049804688
- lengths: int32 [32], P(('dp', 'section')), may hold values from 1 to 128, as said below
- group_ids: int32 [32], P(('dp', 'section')), may hold values from 0 to 3, as said below
- routes: int32 [4096, 1], P(('dp', 'section')), may hold values from 0 to 3; in each aligned block of 256 rows (0 to 255, 256 to 511, ...) at most 80 rows name the same one
- reward_head: bfloat16 [8192], P('mp'), may hold values from -0.0625 to 0.0625
- policy_k: bfloat16 [8192, 256], P(('dp', 'section'), 'mp'), may hold values from -0.0625 to 0.0625
- reference_k: bfloat16 [8192, 256], P(('dp', 'section'), 'mp'), may hold values from -0.0625 to 0.0625
Outputs:
- grad_k: float32 [8192, 256], P(('dp', 'section'), 'mp')
- packed_logp: float32 [4, 4, 320], P('dp', 'section')
The draws below stay inside these ranges and needn't reach their ends.
Inputs may be any that keep to these rules, and one draw needn't show every extreme that they name: `lengths`: some response has all 128 tokens valid. `group_ids`: each prompt id is held by exactly 8 responses. `routes`: among the rows of one rollout device at most 80 name the same learner shard, a bound that some block reaches of them.
All inputs are finite; a program needn't handle non-finite values.
Results may differ from the reference program's by a relative error of at most 0.004.
Values may be sent and summed in bfloat16 or wider, within the bound.
A program may use at most 64 MiB of HBM per device.

```python
import math
import jax
import jax.numpy as jnp
import numpy as np
from jax import lax

D = 8192
SEQ_LEN = 128
GROUP = 8
KVW = 256
TOK_DEV = 256
NSEQ = 32
ROWS = 4096
NGROUPS = 4
CAP = 80
N_DP = 4
N_SECTION = 4


def draw_lengths(key, part):
    key_values, key_spot = jax.random.split(key)
    values = jax.random.randint(key_values, (NSEQ,), 1, SEQ_LEN + 1)
    spot = jax.random.randint(key_spot, (), 0, NSEQ)
    return values.at[spot].set(SEQ_LEN).astype(jnp.int32)


def draw_group_ids(key, part):
    return (jax.random.permutation(key, NSEQ) // GROUP).astype(jnp.int32)


def block_levels(key, dims, shards, least, high):
    factor_of = 1.0
    for axis_at, shards_of in shards:
        heights = jax.random.uniform(jax.random.fold_in(jax.random.fold_in(key, 6), axis_at), (shards_of,), jnp.float32, least / len(shards), high / len(shards))
        factor_of = factor_of * jnp.repeat(jnp.exp(heights), dims[axis_at] // shards_of).reshape((-1,) + (1,) * (len(dims) - 1 - axis_at))
    return factor_of


def shared_out(stream_key, own, number, rows, amount, top, limit, lean):
    ranking = jax.random.permutation(stream_key, amount)
    heavy_load, common = load_shares(amount, rows * top, limit, lean, True), load_shares(amount, rows * top, limit, lean, False)
    places = jnp.arange(amount)

    def named(tallies, offset_by):
        used = int((tallies > 0).sum())
        fixed = max(1, used // 4)
        shifted = fixed + (places - fixed + offset_by * (used - fixed)) % max(1, amount - fixed)
        return jnp.zeros((amount,), jnp.int32).at[ranking[jnp.where(places < fixed, places, shifted)]].set(jnp.asarray(tallies, jnp.int32))

    tallies = jnp.where(number % 4 == 0, named(heavy_load, number // 4), named(common, number - number // 4 - 1))
    mixed = jax.random.permutation(jax.random.fold_in(own, 3), amount)
    source_of, receiver = mixed[0:amount // 2 * 2:2], mixed[1:amount // 2 * 2:2]
    room = jnp.minimum(tallies[source_of] - 1, limit - tallies[receiver]) // 2
    room = jnp.where((source_of == ranking[0]) | (receiver == ranking[0]) | (tallies[receiver] == 0), 0, jnp.maximum(room, 0))
    shifted = jax.random.randint(jax.random.fold_in(own, 4), (amount // 2,), 0, 1 << 20) % (room + 1)
    tallies = tallies.at[source_of].add(-shifted).at[receiver].add(shifted)
    items = jnp.searchsorted(jnp.cumsum(tallies), jnp.arange(rows * top), side="right").astype(jnp.int32)
    listing = items.reshape(top, rows).T
    listing = listing[jax.random.permutation(jax.random.fold_in(own, 1), rows)]
    offset_by = jax.random.randint(jax.random.fold_in(own, 2), (rows, 1), 0, top)
    return jnp.take_along_axis(listing, (jnp.arange(top)[None, :] + offset_by) % top, axis=1)


def load_shares(amount, total, bound, slope, full):
    portions = [(1 << 20) // math.isqrt(grade ** slope) + 1 for grade in range(1, amount + 1)]
    largest = bound if full else min(bound, max(-(-total // amount), total * portions[0] // sum(portions)))
    least = 1 if total - largest >= amount - 1 else 0
    holding, spare = [largest] + [least] * (amount - 1), total - largest - least * (amount - 1)
    while spare > 0:
        free = [i for i in range(1, amount) if holding[i] < largest] or [i for i in range(1, amount) if holding[i] < bound]
        mass, remaining = sum([portions[i] for i in free]), spare
        for i in free:
            more = min(bound - holding[i], max(1, remaining * portions[i] // mass), spare)
            holding[i] = holding[i] + more
            spare = spare - more
    return np.array(holding)


def centred(stream_key, shape, deviation, bound, cuts=(), held_as=jnp.bfloat16):
    array = deviation * jax.random.normal(stream_key, shape, jnp.float32)
    if cuts:
        array = array * block_levels(stream_key, shape, cuts, -0.22, 0.18)
    return jnp.clip(array, -bound, bound).astype(held_as)


def setup_inputs(seed: int = 0) -> dict:
    arg_keys = jax.random.split(jax.random.key(seed), 10)
    states = centred(arg_keys[0], (ROWS, D), 1.0, 6.0, ((0, 16), (1, 2)))
    direction = centred(arg_keys[1], (ROWS, KVW), (4 * KVW) ** -0.5, 0.1875, ((0, 16), (1, 2)))
    old_logp = jnp.clip(-4.0 + 3.9501953 * jax.random.uniform(arg_keys[2], (ROWS,), jnp.float32) ** block_levels(arg_keys[2], (ROWS,), ((0, 16),), -0.2, 0.2), -4.0, -0.049804688).astype(jnp.bfloat16)
    lengths = draw_lengths(jax.random.fold_in(arg_keys[9], 71), 0)
    group_ids = draw_group_ids(jax.random.fold_in(arg_keys[9], 71), 0)
    routes_keys = jax.random.split(jax.random.fold_in(arg_keys[5], 1), ROWS // TOK_DEV)
    routes_turns = jax.random.permutation(jax.random.fold_in(arg_keys[5], 3), ROWS // TOK_DEV)
    routes = jax.vmap(lambda own, number: shared_out(jax.random.fold_in(arg_keys[5], 2), own, number, TOK_DEV, N_DP, 1, CAP, 2))(routes_keys, routes_turns).reshape((ROWS, 1))
    reward_head = centred(arg_keys[6], (D,), D ** -0.5, 0.0625, ((0, 2),))
    policy_k = centred(arg_keys[7], (D, KVW), D ** -0.5, 0.0625, ((0, 16), (1, 2)))
    reference_k = centred(arg_keys[8], (D, KVW), D ** -0.5, 0.0625, ((0, 16), (1, 2)))
    return dict(states=states, direction=direction, old_logp=old_logp, lengths=lengths, group_ids=group_ids, routes=routes, reward_head=reward_head, policy_k=policy_k, reference_k=reference_k)


kl_weight = 0.4
var_offset = 0.25

def reference(states, direction, old_logp, lengths, group_ids, routes, reward_head, policy_k, reference_k):
    score = jnp.dot(states, reward_head, preferred_element_type=jnp.float32)
    valid = (jnp.arange(SEQ_LEN, dtype=jnp.int32)[None, :] < lengths[:, None]).astype(jnp.float32)
    reward = lax.optimization_barrier(jnp.sum(score.reshape(NSEQ, SEQ_LEN) * valid, axis=1)) / jnp.sqrt(lengths.astype(jnp.float32))
    member = (group_ids[:, None] == jnp.arange(NGROUPS, dtype=jnp.int32)[None, :]).astype(jnp.float32)
    totals = lax.optimization_barrier(jnp.sum(member * reward[:, None], axis=0))
    squares = lax.optimization_barrier(jnp.sum(member * (reward * reward)[:, None], axis=0))
    center = totals / GROUP
    spread = squares / GROUP - center * center
    own_center = lax.optimization_barrier(jnp.sum(member * center[None, :], axis=1))
    own_spread = lax.optimization_barrier(jnp.sum(member * spread[None, :], axis=1))
    advantage = ((reward - own_center) / jnp.sqrt(own_spread + var_offset)).astype(jnp.bfloat16)
    key_policy = jnp.dot(states, policy_k, preferred_element_type=jnp.float32)
    key_reference = jnp.dot(states, reference_k, preferred_element_type=jnp.float32)
    dir_wide = direction.astype(jnp.float32)
    term_policy = lax.optimization_barrier(jnp.sum(dir_wide * key_policy, axis=1))
    term_reference = lax.optimization_barrier(jnp.sum(dir_wide * key_reference, axis=1))
    logp = old_logp.astype(jnp.float32) + term_policy
    adv_rows = jnp.repeat(advantage.astype(jnp.float32), SEQ_LEN)
    valid_rows = valid.reshape(ROWS)
    coef = valid_rows * (-adv_rows * jnp.exp(term_policy) + kl_weight * (1.0 - jnp.exp(term_reference - term_policy)))
    change = (coef[:, None] * dir_wide).astype(jnp.bfloat16)
    grad_k = jnp.dot(states.T, change, preferred_element_type=jnp.float32)
    target = routes[:, 0]
    blocks = N_DP * N_SECTION
    choose = (target.reshape(blocks, TOK_DEV)[:, :, None] == jnp.arange(N_DP, dtype=jnp.int32)[None, None, :]).astype(jnp.int32)
    ranked = jnp.cumsum(choose, axis=1) - 1
    within = lax.optimization_barrier(jnp.sum(ranked * choose, axis=2)).reshape(ROWS)
    block_of = jnp.arange(ROWS, dtype=jnp.int32) // TOK_DEV
    source_dp = block_of // N_SECTION
    section_of = block_of % N_SECTION
    packed_logp = jnp.zeros((N_DP, N_SECTION, N_DP * CAP), jnp.float32)
    packed_logp = packed_logp.at[target, section_of, source_dp * CAP + within].set(logp)
    return (grad_k, packed_logp)
```

```python
import functools

import jax
import jax.numpy as jnp
from jax import lax
from jax.experimental import pallas as pl
from jax.experimental.pallas import tpu as pltpu
from jax.sharding import PartitionSpec as P

GROUP = 8
kl_weight = 0.4
var_offset = 0.25
F32 = jnp.float32
BF16 = jnp.bfloat16
MESH = pl.DeviceIdType.MESH
LAST = (((1,), (1,)), ((), ()))


def kernel(
    N, M, S, cap, width,
    states, dirs, old, lens, gids, routes, head, pol, ref,
    grad, pack,
    own, sbuf, ksend, kt, dbuf, msg1, msg2, rgl, tbuf, tsum, hot, chg, gsend, grecv, psend, precv,
    own_sem, s_send, s_recv, k_send, k_recv, d_send, d_recv, m1_send, m1_recv, m2_send, m2_recv,
    t_send, t_recv, g_send, g_recv, p_send, p_recv,
):
    z, m, s = lax.axis_index("dp"), lax.axis_index("mp"), lax.axis_index("section")
    per = N // M
    T = states.shape[0]
    nl = lens.shape[0]
    L = T // nl
    Q = S * nl
    F, C = pol.shape

    def at(zz, mm, ss):
        return {"dp": zz, "mp": mm, "section": ss}

    def remote(src, dst, send, recv, to):
        return pltpu.make_async_remote_copy(
            src_ref=src, dst_ref=dst, send_sem=send, recv_sem=recv, device_id=to, device_id_type=MESH
        )

    def landed(dst, sem):
        pltpu.make_async_copy(dst, dst, sem).wait()

    plane = [
        (k, (m + k % M) % M, (s + k // M) % S) for k in range(1, S * M)
    ]
    column = [((z + dz) % N, (m + dm) % M) for dz in range(1, N) for dm in range(M)]

    barrier = pltpu.get_barrier_semaphore()
    for _, mm, ss in plane:
        pl.semaphore_signal(barrier, inc=1, device_id=at(z, mm, ss), device_id_type=MESH)
    for zz, mm in column:
        pl.semaphore_signal(barrier, inc=1, device_id=at(zz, mm, s), device_id_type=MESH)

    own_copy = pltpu.make_async_copy(states, own, own_sem)
    own_copy.start()

    def columns(ii, ss):
        return states.at[:, pl.ds(pl.multiple_of((S * ii + ss) * F, F), F)]

    for ii in range(per):
        pltpu.make_async_copy(columns(ii, s), sbuf.at[ii, s], s_recv.at[ii, s]).start()
    ksend[0:C, :] = pol[...].astype(F32).T.astype(BF16)
    ksend[C : 2 * C, :] = ref[...].astype(F32).T.astype(BF16)
    dbuf[s, m] = dirs[...].astype(F32).T.astype(BF16)

    pl.semaphore_wait(barrier, S * M - 1 + (N - 1) * M)

    sent = []

    def go(copy):
        copy.start()
        sent.append(copy)

    for k, mm, ss in plane:
        go(remote(dbuf.at[s, m], dbuf.at[s, m], d_send.at[k], d_recv.at[s, m], at(z, mm, ss)))
    m_k = z // per
    k_slot = kt.at[z % per, m]
    k_sem = k_recv.at[z % per, m]
    order = [(ds, ii) for ii in range(per) for ds in range(1, S)]
    for n in range(max(len(order), N - 1)):
        if n < len(order):
            ds, ii = order[n]
            ss = (s + ds) % S
            go(remote(columns(ii, ss), sbuf.at[ii, s], s_send.at[ii, ds], s_recv.at[ii, s], at(z, m, ss)))
        if n < N - 1:
            dz = n + 1
            go(remote(ksend, k_slot, k_send.at[dz], k_sem, at((z + dz) % N, m_k, s)))
    k_near = remote(ksend, k_slot, k_send.at[0], k_sem, at(z, m_k, s))

    @pl.when(m_k != m)
    def _():
        k_near.start()

    @pl.when(m_k == m)
    def _():
        pltpu.make_async_copy(ksend, k_slot, k_sem).start()

    own_copy.wait()
    scores = lax.dot_general(
        jnp.broadcast_to(head[...], (16, head.shape[1])), own[...], LAST, preferred_element_type=F32
    )[0:1, :]
    spot = lax.broadcasted_iota(jnp.int32, (1, L), 1)
    for r in range(nl):
        mine = jnp.where(spot < lens[r], scores[:, r * L : (r + 1) * L], 0.0)
        msg1[s, m, r : r + 1, :] = jnp.broadcast_to(jnp.sum(mine, axis=1, keepdims=True), (1, 128))
        msg1[s, m, nl + r : nl + r + 1, :] = jnp.full((1, 128), lens[r].astype(F32))
        msg1[s, m, 2 * nl + r : 2 * nl + r + 1, :] = jnp.full((1, 128), gids[r].astype(F32))
    for k, mm, ss in plane:
        go(remote(msg1.at[s, m], msg1.at[s, m], m1_send.at[k], m1_recv.at[s, m], at(z, mm, ss)))

    rows = max(16, N)
    shard = lax.broadcasted_iota(jnp.int32, (rows, T), 0)
    choose = (shard == routes[...]).astype(F32)
    upto = (
        lax.broadcasted_iota(jnp.int32, (T, T), 0) <= lax.broadcasted_iota(jnp.int32, (T, T), 1)
    ).astype(F32).astype(BF16)
    ranked = jnp.dot(choose.astype(BF16), upto, preferred_element_type=F32) - 1.0
    within = jnp.sum(ranked * choose, axis=0, keepdims=True)
    slot = routes[...].astype(F32) * width + within + (z * cap).astype(F32)
    for r in range(N):
        place = lax.broadcasted_iota(jnp.int32, (width, T), 0).astype(F32) + float(r * width)
        hot[r * width : (r + 1) * width, :] = (place == slot).astype(F32).astype(BF16)

    for k, mm, ss in plane:
        landed(msg1.at[ss, mm], m1_recv.at[ss, mm])
    for t in range(S):
        total = msg1[t, 0, 0:nl, :]
        for mm in range(1, M):
            total = total + msg1[t, mm, 0:nl, :]
        rgl[0, t * nl : (t + 1) * nl, :] = total
        rgl[1, t * nl : (t + 1) * nl, :] = msg1[t, 0, nl : 2 * nl, :]
        rgl[2, t * nl : (t + 1) * nl, :] = msg1[t, 0, 2 * nl : 3 * nl, :]
    reward = rgl[0] / jnp.sqrt(rgl[1])
    lane = lax.broadcasted_iota(jnp.int32, (Q, 128), 1).astype(F32)
    member = rgl[2] == lane
    held = jnp.where(member, reward, 0.0)
    msg2[z, 0:1, :] = jnp.sum(held, axis=0, keepdims=True)
    msg2[z, 1:2, :] = jnp.sum(held * held, axis=0, keepdims=True)
    msg2[z, 2:8, :] = jnp.zeros((6, 128), F32)
    for dz in range(1, N):
        go(remote(msg2.at[z], msg2.at[z], m2_send.at[dz], m2_recv.at[z], at((z + dz) % N, m, s)))
    for dz in range(1, N):
        landed(msg2.at[(z + dz) % N], m2_recv.at[(z + dz) % N])
    sums = msg2[0]
    for zz in range(1, N):
        sums = sums + msg2[zz]
    center = sums[0:1, :] / GROUP
    spread = sums[1:2, :] / GROUP - center * center
    own_center = jnp.sum(jnp.where(member, center, 0.0), axis=1, keepdims=True)
    own_spread = jnp.sum(jnp.where(member, spread, 0.0), axis=1, keepdims=True)
    advantage = ((reward - own_center) / jnp.sqrt(own_spread + var_offset)).astype(BF16).astype(F32)
    valid = (
        lax.broadcasted_iota(jnp.int32, (Q, L), 1).astype(F32) < rgl[1][:, 0:1]
    ).astype(F32)

    for k, mm, ss in plane:
        landed(dbuf.at[ss, mm], d_recv.at[ss, mm])
    for ii in range(per):
        for mm in range(M):
            landed(kt.at[ii, mm], k_recv.at[ii, mm])

    for t in range(S):
        keys = None
        for ii in range(per):
            landed(sbuf.at[ii, t], s_recv.at[ii, t])
            part = lax.dot_general(
                kt[ii].reshape(2 * M * C, F), sbuf[ii, t], LAST, preferred_element_type=F32
            )
            keys = part if keys is None else keys + part
        for which in range(2):
            term = None
            for mm in range(M):
                low = (2 * mm + which) * C
                part = jnp.sum(dbuf[t, mm].astype(F32) * keys[low : low + C, :], axis=0, keepdims=True)
                term = part if term is None else term + part
            for r in range(nl):
                q = t * nl + r
                tbuf[s, m, which, q : q + 1, :] = term[:, r * L : (r + 1) * L]
    for k, mm, ss in plane:
        go(remote(tbuf.at[s, m], tbuf.at[s, m], t_send.at[k], t_recv.at[s, m], at(z, mm, ss)))
    for k, mm, ss in plane:
        landed(tbuf.at[ss, mm], t_recv.at[ss, mm])
    terms = None
    for t in range(S):
        for mm in range(M):
            terms = tbuf[t, mm] if terms is None else terms + tbuf[t, mm]
    tp, tr = terms[0], terms[1]
    coef = valid * (-advantage * jnp.exp(tp) + kl_weight * (1.0 - jnp.exp(tr - tp)))
    for q in range(Q):
        t, r = q // nl, q % nl
        for mm in range(M):
            chg[mm * C : (mm + 1) * C, q * L : (q + 1) * L] = (
                dbuf[t, mm, :, r * L : (r + 1) * L].astype(F32) * coef[q : q + 1, :]
            ).astype(BF16)
    g_near = []
    for ii in range(per):
        part = jnp.dot(chg[...], sbuf[ii].reshape(S * T, F), preferred_element_type=F32)
        for mm in range(M):
            gsend[ii, mm] = part[mm * C : (mm + 1) * C, :].astype(BF16)
        zz = m * per + ii
        for dm in range(1, M):
            mm = (m + dm) % M
            go(remote(gsend.at[ii, mm], grecv.at[z], g_send.at[ii, dm], g_recv.at[z], at(zz, mm, s)))
        far = remote(gsend.at[ii, m], grecv.at[z], g_send.at[ii, 0], g_recv.at[z], at(zz, m, s))
        g_near.append((zz, far))

        @pl.when(zz != z)
        def _(far=far):
            far.start()

        @pl.when(zz == z)
        def _(ii=ii):
            pltpu.make_async_copy(gsend.at[ii, m], grecv.at[z], g_recv.at[z]).start()

    tsum[...] = tp
    logp = old[...] + tsum[pl.ds(s * nl, nl), :]
    row = jnp.concatenate([logp[r : r + 1, :] for r in range(nl)], axis=1)
    high = row.astype(BF16).astype(F32)
    mid = (row - high).astype(BF16).astype(F32)
    low = row - high - mid
    split = jnp.concatenate([high, mid, low, jnp.zeros((13, T), F32)], axis=0).astype(BF16)
    placed = lax.dot_general(split, hot[...], LAST, preferred_element_type=F32)
    line = placed[0:1, :] + placed[1:2, :] + placed[2:3, :]
    for r in range(N):
        psend[r] = jnp.broadcast_to(line[:, r * width : (r + 1) * width], (8, width))
    for dz in range(1, N):
        zz = (z + dz) % N
        go(remote(psend.at[zz], precv.at[z], p_send.at[dz], p_recv.at[z], at(zz, m, s)))
    precv[z] = psend[z]
    for dz in range(1, N):
        landed(precv.at[(z + dz) % N], p_recv.at[(z + dz) % N])
    packed = precv[0]
    for zz in range(1, N):
        packed = packed + precv[zz]
    pack[0] = packed[0:1, : N * cap]

    total = None
    for zz in range(N):
        landed(grecv.at[zz], g_recv.at[zz])
        part = grecv[zz].astype(F32)
        total = part if total is None else total + part
    grad[...] = total.T

    for copy in sent:
        copy.wait_send()

    @pl.when(m_k != m)
    def _():
        k_near.wait_send()

    for zz, far in g_near:

        @pl.when(zz != z)
        def _(far=far):
            far.wait_send()


def body(states, direction, old_logp, lengths, group_ids, routes, reward_head, policy_k, reference_k):
    N, M, S = lax.axis_size("dp"), lax.axis_size("mp"), lax.axis_size("section")
    T = states.shape[0]
    nl = lengths.shape[0]
    L = T // nl
    F, C = policy_k.shape
    per = N // M
    Q = S * nl
    cap = max(2, 5 * T // (4 * N))
    width = -(-N * cap // 128) * 128
    vm = pl.BlockSpec(memory_space=pltpu.VMEM)
    sm = pl.BlockSpec(memory_space=pltpu.SMEM)
    dma = pltpu.SemaphoreType.DMA
    high = -(-3 * nl // 8) * 8
    grad_k, packed = pl.pallas_call(
        functools.partial(kernel, N, M, S, cap, width),
        out_shape=(
            jax.ShapeDtypeStruct((F, C), F32),
            jax.ShapeDtypeStruct((1, 1, N * cap), F32),
        ),
        in_specs=[pl.BlockSpec(memory_space=pl.ANY), vm, vm, sm, sm, vm, vm, vm, vm],
        out_specs=(vm, vm),
        scratch_shapes=[
            pltpu.VMEM(states.shape, BF16),
            pltpu.VMEM((per, S, T, F), BF16),
            pltpu.VMEM((2 * C, F), BF16),
            pltpu.VMEM((per, M, 2 * C, F), BF16),
            pltpu.VMEM((S, M, C, T), BF16),
            pltpu.VMEM((S, M, high, 128), F32),
            pltpu.VMEM((N, 8, 128), F32),
            pltpu.VMEM((3, Q, 128), F32),
            pltpu.VMEM((S, M, 2, Q, L), F32),
            pltpu.VMEM((Q, L), F32),
            pltpu.VMEM((N * width, T), BF16),
            pltpu.VMEM((M * C, S * T), BF16),
            pltpu.VMEM((per, M, C, F), BF16),
            pltpu.VMEM((N, C, F), BF16),
            pltpu.VMEM((N, 8, width), F32),
            pltpu.VMEM((N, 8, width), F32),
            dma,
            dma((per, S)), dma((per, S)),
            dma((N,)), dma((per, M)),
            dma((S * M,)), dma((S, M)),
            dma((S * M,)), dma((S, M)),
            dma((N,)), dma((N,)),
            dma((S * M,)), dma((S, M)),
            dma((per, M)), dma((N,)),
            dma((N,)), dma((N,)),
        ],
        compiler_params=pltpu.CompilerParams(
            collective_id=0, has_side_effects=True, vmem_limit_bytes=48 * 1024 * 1024
        ),
    )(
        states,
        direction,
        old_logp.astype(F32).reshape(nl, L),
        lengths,
        group_ids,
        routes.reshape(1, T),
        reward_head.reshape(1, -1),
        policy_k,
        reference_k,
    )
    return grad_k, packed


def solution(mesh):
    both = ("dp", "section")
    return jax.shard_map(
        body,
        mesh=mesh,
        in_specs=(
            P(both, "mp"),
            P(both, "mp"),
            P(both),
            P(both),
            P(both),
            P(both, None),
            P("mp"),
            P(both, "mp"),
            P(both, "mp"),
        ),
        out_specs=(P(both, "mp"), P("dp", "section", None)),
        check_vma=False,
    )
```

```python
import functools

import jax
import jax.numpy as jnp
from jax import lax
from jax.experimental import pallas as pl
from jax.experimental.pallas import tpu as pltpu
from jax.sharding import PartitionSpec as P

GROUP = 8
kl_weight = 0.4
var_offset = 0.25
F32 = jnp.float32
BF16 = jnp.bfloat16
MESH = pl.DeviceIdType.MESH
LAST = (((1,), (1,)), ((), ()))


def kernel(
    N, M, S, cap, width,
    states, dirs_in, old_in, lens_in, gids_in, routes_in, head_in, pol_in, ref_in,
    grad, pack,
    dirs, old, lens, gids, routes, head, pol, ref, in_sem,
    own, sbuf, ksend, kt, dbuf, msg1, msg2, rgl, tbuf, tsum, hot, chg, gsend, grecv, psend, precv,
    own_sem, s_send, s_recv, k_send, k_recv, d_send, d_recv, m1_send, m1_recv, m2_send, m2_recv,
    t_send, t_recv, g_send, g_recv, p_send, p_recv,
):
    z, m, s = lax.axis_index("dp"), lax.axis_index("mp"), lax.axis_index("section")
    per = N // M
    T = states.shape[0]
    nl = lens_in.shape[0]
    L = T // nl
    Q = S * nl
    F, C = pol_in.shape

    def at(zz, mm, ss):
        return {"dp": zz, "mp": mm, "section": ss}

    def remote(src, dst, send, recv, to):
        return pltpu.make_async_remote_copy(
            src_ref=src, dst_ref=dst, send_sem=send, recv_sem=recv, device_id=to, device_id_type=MESH
        )

    def landed(dst, sem):
        pltpu.make_async_copy(dst, dst, sem).wait()

    plane = [
        (k, (m + k % M) % M, (s + k // M) % S) for k in range(1, S * M)
    ]
    column = [((z + dz) % N, (m + dm) % M) for dz in range(1, N) for dm in range(M)]

    barrier = pltpu.get_barrier_semaphore()
    for _, mm, ss in plane:
        pl.semaphore_signal(barrier, inc=1, device_id=at(z, mm, ss), device_id_type=MESH)
    for zz, mm in column:
        pl.semaphore_signal(barrier, inc=1, device_id=at(zz, mm, s), device_id_type=MESH)

    loads = [
        pltpu.make_async_copy(src, dst, in_sem.at[n])
        for n, (src, dst) in enumerate(
            (
                (dirs_in, dirs), (pol_in, pol), (ref_in, ref), (head_in, head),
                (lens_in, lens), (gids_in, gids), (routes_in, routes), (old_in, old),
            )
        )
    ]
    for load in loads:
        load.start()
    own_copy = pltpu.make_async_copy(states, own, own_sem)
    own_copy.start()

    def columns(ii, ss):
        return states.at[:, pl.ds(pl.multiple_of((S * ii + ss) * F, F), F)]

    for ii in range(per):
        pltpu.make_async_copy(columns(ii, s), sbuf.at[ii, s], s_recv.at[ii, s]).start()
    loads[0].wait()
    dbuf[s, m] = dirs[...].astype(F32).T.astype(BF16)

    pl.semaphore_wait(barrier, S * M - 1 + (N - 1) * M)

    sent = []

    def go(copy):
        copy.start()
        sent.append(copy)

    for ds in range(1, S):
        ss = (s + ds) % S
        go(remote(dbuf.at[s, m], dbuf.at[s, m], d_send.at[0, ds], d_recv.at[s, m], at(z, m, ss)))
    for ii in range(per):
        for ds in range(1, S):
            ss = (s + ds) % S
            go(remote(columns(ii, ss), sbuf.at[ii, s], s_send.at[ii, ds], s_recv.at[ii, s], at(z, m, ss)))
    for load in loads[1:3]:
        load.wait()
    ksend[0:C, :] = pol[...].astype(F32).T.astype(BF16)
    ksend[C : 2 * C, :] = ref[...].astype(F32).T.astype(BF16)
    m_k = z // per
    k_slot = kt.at[z % per, m]
    k_sem = k_recv.at[z % per, m]
    for dz in range(1, N):
        go(remote(ksend, k_slot, k_send.at[dz], k_sem, at((z + dz) % N, m_k, s)))
    k_near = remote(ksend, k_slot, k_send.at[0], k_sem, at(z, m_k, s))

    @pl.when(m_k != m)
    def _():
        k_near.start()

    @pl.when(m_k == m)
    def _():
        pltpu.make_async_copy(ksend, k_slot, k_sem).start()

    for load in loads[3:]:
        load.wait()
    own_copy.wait()
    scores = lax.dot_general(
        jnp.broadcast_to(head[...].reshape(1, -1), (16, head.shape[0])), own[...], LAST, preferred_element_type=F32
    )[0:1, :]
    spot = lax.broadcasted_iota(jnp.int32, (1, L), 1)
    for r in range(nl):
        mine = jnp.where(spot < lens[r], scores[:, r * L : (r + 1) * L], 0.0)
        msg1[s, m, r : r + 1, :] = jnp.broadcast_to(jnp.sum(mine, axis=1, keepdims=True), (1, 128))
        msg1[s, m, nl + r : nl + r + 1, :] = jnp.full((1, 128), lens[r].astype(F32))
        msg1[s, m, 2 * nl + r : 2 * nl + r + 1, :] = jnp.full((1, 128), gids[r].astype(F32))
    for k, mm, ss in plane:
        go(remote(msg1.at[s, m], msg1.at[s, m], m1_send.at[k], m1_recv.at[s, m], at(z, mm, ss)))

    for ds in range(S):
        ss = (s + ds) % S
        if ds:
            landed(dbuf.at[ss, m], d_recv.at[ss, m])
        for dm in range(1, M):
            to = at(z, (m + dm) % M, s)
            go(remote(dbuf.at[ss, m], dbuf.at[ss, m], d_send.at[dm, ds], d_recv.at[ss, m], to))

    rows = max(16, N)
    shard = lax.broadcasted_iota(jnp.int32, (rows, T), 0)
    choose = (shard == routes[...]).astype(F32)
    upto = (
        lax.broadcasted_iota(jnp.int32, (T, T), 0) <= lax.broadcasted_iota(jnp.int32, (T, T), 1)
    ).astype(F32).astype(BF16)
    ranked = jnp.dot(choose.astype(BF16), upto, preferred_element_type=F32) - 1.0
    within = jnp.sum(ranked * choose, axis=0, keepdims=True)
    slot = routes[...].astype(F32) * width + within + (z * cap).astype(F32)
    for r in range(N):
        place = lax.broadcasted_iota(jnp.int32, (width, T), 0).astype(F32) + float(r * width)
        hot[r * width : (r + 1) * width, :] = (place == slot).astype(F32).astype(BF16)

    for k, mm, ss in plane:
        landed(msg1.at[ss, mm], m1_recv.at[ss, mm])
    for t in range(S):
        total = msg1[t, 0, 0:nl, :]
        for mm in range(1, M):
            total = total + msg1[t, mm, 0:nl, :]
        rgl[0, t * nl : (t + 1) * nl, :] = total
        rgl[1, t * nl : (t + 1) * nl, :] = msg1[t, 0, nl : 2 * nl, :]
        rgl[2, t * nl : (t + 1) * nl, :] = msg1[t, 0, 2 * nl : 3 * nl, :]
    reward = rgl[0] / jnp.sqrt(rgl[1])
    lane = lax.broadcasted_iota(jnp.int32, (Q, 128), 1).astype(F32)
    member = rgl[2] == lane
    held = jnp.where(member, reward, 0.0)
    msg2[z, 0:1, :] = jnp.sum(held, axis=0, keepdims=True)
    msg2[z, 1:2, :] = jnp.sum(held * held, axis=0, keepdims=True)
    msg2[z, 2:8, :] = jnp.zeros((6, 128), F32)
    for dz in range(1, N):
        go(remote(msg2.at[z], msg2.at[z], m2_send.at[dz], m2_recv.at[z], at((z + dz) % N, m, s)))
    for dz in range(1, N):
        landed(msg2.at[(z + dz) % N], m2_recv.at[(z + dz) % N])
    sums = msg2[0]
    for zz in range(1, N):
        sums = sums + msg2[zz]
    center = sums[0:1, :] / GROUP
    spread = sums[1:2, :] / GROUP - center * center
    own_center = jnp.sum(jnp.where(member, center, 0.0), axis=1, keepdims=True)
    own_spread = jnp.sum(jnp.where(member, spread, 0.0), axis=1, keepdims=True)
    advantage = ((reward - own_center) / jnp.sqrt(own_spread + var_offset)).astype(BF16).astype(F32)
    valid = (
        lax.broadcasted_iota(jnp.int32, (Q, L), 1).astype(F32) < rgl[1][:, 0:1]
    ).astype(F32)

    for ii in range(per):
        for mm in range(M):
            landed(kt.at[ii, mm], k_recv.at[ii, mm])
    for ds in range(S):
        for dm in range(1, M):
            ss, mm = (s + ds) % S, (m + dm) % M
            landed(dbuf.at[ss, mm], d_recv.at[ss, mm])

    for ds in range(S):
        t = (s + ds) % S
        keys = None
        for ii in range(per):
            landed(sbuf.at[ii, t], s_recv.at[ii, t])
            part = lax.dot_general(
                kt[ii].reshape(2 * M * C, F), sbuf[ii, t], LAST, preferred_element_type=F32
            )
            keys = part if keys is None else keys + part
        for which in range(2):
            term = None
            for mm in range(M):
                low = (2 * mm + which) * C
                part = jnp.sum(dbuf[t, mm].astype(F32) * keys[low : low + C, :], axis=0, keepdims=True)
                term = part if term is None else term + part
            for r in range(nl):
                n = which * nl + r
                tbuf[s, m, t, n : n + 1, :] = term[:, r * L : (r + 1) * L]
    for k, mm, ss in plane:
        go(remote(tbuf.at[s, m], tbuf.at[s, m], t_send.at[k], t_recv.at[s, m], at(z, mm, ss)))
    for k, mm, ss in plane:
        landed(tbuf.at[ss, mm], t_recv.at[ss, mm])
    for t in range(S):
        terms = None
        for ss in range(S):
            for mm in range(M):
                terms = tbuf[ss, mm, t] if terms is None else terms + tbuf[ss, mm, t]
        tp, tr = terms[0:nl, :], terms[nl : 2 * nl, :]
        tsum[t] = tp
        adv = advantage[t * nl : (t + 1) * nl, :]
        coef = valid[t * nl : (t + 1) * nl, :] * (
            -adv * jnp.exp(tp) + kl_weight * (1.0 - jnp.exp(tr - tp))
        )
        for r in range(nl):
            q = t * nl + r
            for mm in range(M):
                chg[mm * C : (mm + 1) * C, q * L : (q + 1) * L] = (
                    dbuf[t, mm, :, r * L : (r + 1) * L].astype(F32) * coef[r : r + 1, :]
                ).astype(BF16)
    g_near = []
    for ii in range(per):
        part = jnp.dot(chg[...], sbuf[ii].reshape(S * T, F), preferred_element_type=F32)
        for mm in range(M):
            gsend[ii, mm] = part[mm * C : (mm + 1) * C, :].astype(BF16)
        zz = m * per + ii
        for dm in range(1, M):
            mm = (m + dm) % M
            go(remote(gsend.at[ii, mm], grecv.at[z], g_send.at[ii, dm], g_recv.at[z], at(zz, mm, s)))
        far = remote(gsend.at[ii, m], grecv.at[z], g_send.at[ii, 0], g_recv.at[z], at(zz, m, s))
        g_near.append((zz, far))

        @pl.when(zz != z)
        def _(far=far):
            far.start()

        @pl.when(zz == z)
        def _(ii=ii):
            pltpu.make_async_copy(gsend.at[ii, m], grecv.at[z], g_recv.at[z]).start()

        if ii == 0:
            logp = tsum[s]
            row = jnp.concatenate([logp[r : r + 1, :] for r in range(nl)], axis=1) + old[...].reshape(1, T).astype(F32)
            high = row.astype(BF16).astype(F32)
            mid = (row - high).astype(BF16).astype(F32)
            low = row - high - mid
            split = jnp.concatenate([high, mid, low, jnp.zeros((13, T), F32)], axis=0).astype(BF16)
            placed = lax.dot_general(split, hot[...], LAST, preferred_element_type=F32)
            line = placed[0:1, :] + placed[1:2, :] + placed[2:3, :]
            for r in range(N):
                psend[r] = line[:, r * width : (r + 1) * width]
            for dz in range(1, N):
                zz = (z + dz) % N
                go(remote(psend.at[zz], precv.at[z], p_send.at[dz], p_recv.at[z], at(zz, m, s)))

    precv[z] = psend[z]
    for dz in range(1, N):
        landed(precv.at[(z + dz) % N], p_recv.at[(z + dz) % N])
    packed = precv[0]
    for zz in range(1, N):
        packed = packed + precv[zz]
    pack[0] = packed[:, : N * cap]

    total = None
    for zz in range(N):
        landed(grecv.at[zz], g_recv.at[zz])
        part = grecv[zz].astype(F32)
        total = part if total is None else total + part
    grad[...] = total.T

    for copy in sent:
        copy.wait_send()

    @pl.when(m_k != m)
    def _():
        k_near.wait_send()

    for zz, far in g_near:

        @pl.when(zz != z)
        def _(far=far):
            far.wait_send()


def body(states, direction, old_logp, lengths, group_ids, routes, reward_head, policy_k, reference_k):
    N, M, S = lax.axis_size("dp"), lax.axis_size("mp"), lax.axis_size("section")
    T = states.shape[0]
    nl = lengths.shape[0]
    L = T // nl
    F, C = policy_k.shape
    per = N // M
    Q = S * nl
    cap = max(2, 5 * T // (4 * N))
    width = -(-N * cap // 128) * 128
    vm = pl.BlockSpec(memory_space=pltpu.VMEM)
    dma = pltpu.SemaphoreType.DMA
    high = -(-3 * nl // 8) * 8
    grad_k, packed = pl.pallas_call(
        functools.partial(kernel, N, M, S, cap, width),
        out_shape=(
            jax.ShapeDtypeStruct((F, C), F32),
            jax.ShapeDtypeStruct((1, 1, N * cap), F32),
        ),
        in_specs=[pl.BlockSpec(memory_space=pl.ANY)] * 9,
        out_specs=(vm, vm),
        scratch_shapes=[
            pltpu.VMEM(direction.shape, BF16),
            pltpu.VMEM((T,), BF16),
            pltpu.SMEM((nl,), jnp.int32),
            pltpu.SMEM((nl,), jnp.int32),
            pltpu.VMEM((1, T), jnp.int32),
            pltpu.VMEM(reward_head.shape, BF16),
            pltpu.VMEM((F, C), BF16),
            pltpu.VMEM((F, C), BF16),
            dma((8,)),
            pltpu.VMEM(states.shape, BF16),
            pltpu.VMEM((per, S, T, F), BF16),
            pltpu.VMEM((2 * C, F), BF16),
            pltpu.VMEM((per, M, 2 * C, F), BF16),
            pltpu.VMEM((S, M, C, T), BF16),
            pltpu.VMEM((S, M, high, 128), F32),
            pltpu.VMEM((N, 8, 128), F32),
            pltpu.VMEM((3, Q, 128), F32),
            pltpu.VMEM((S, M, S, 2 * nl, L), F32),
            pltpu.VMEM((S, nl, L), F32),
            pltpu.VMEM((N * width, T), BF16),
            pltpu.VMEM((M * C, S * T), BF16),
            pltpu.VMEM((per, M, C, F), BF16),
            pltpu.VMEM((N, C, F), BF16),
            pltpu.VMEM((N, 1, width), F32),
            pltpu.VMEM((N, 1, width), F32),
            dma,
            dma((per, S)), dma((per, S)),
            dma((N,)), dma((per, M)),
            dma((M, S)), dma((S, M)),
            dma((S * M,)), dma((S, M)),
            dma((N,)), dma((N,)),
            dma((S * M,)), dma((S, M)),
            dma((per, M)), dma((N,)),
            dma((N,)), dma((N,)),
        ],
        compiler_params=pltpu.CompilerParams(
            collective_id=0, has_side_effects=True, vmem_limit_bytes=64 * 1024 * 1024
        ),
    )(
        states,
        direction,
        old_logp,
        lengths,
        group_ids,
        routes.reshape(1, T),
        reward_head,
        policy_k,
        reference_k,
    )
    return grad_k, packed


def solution(mesh):
    both = ("dp", "section")
    return jax.shard_map(
        body,
        mesh=mesh,
        in_specs=(
            P(both, "mp"),
            P(both, "mp"),
            P(both),
            P(both),
            P(both),
            P(both, None),
            P("mp"),
            P(both, "mp"),
            P(both, "mp"),
        ),
        out_specs=(P(both, "mp"), P("dp", "section", None)),
        check_vma=False,
    )
```

```python
import functools

import jax
import jax.numpy as jnp
from jax import lax
from jax.experimental import pallas as pl
from jax.experimental.pallas import tpu as pltpu
from jax.sharding import PartitionSpec as P

GROUP = 8
kl_weight = 0.4
var_offset = 0.25
F32 = jnp.float32
BF16 = jnp.bfloat16
MESH = pl.DeviceIdType.MESH
LAST = (((1,), (1,)), ((), ()))


def kernel(
    N, M, S, cap, width,
    states, dirs_in, old_in, lens_in, gids_in, routes_in, head_in, pol_in, ref_in,
    grad, pack,
    dirs, old, lens, gids, routes, head, pol, ref, in_sem,
    own, sbuf, ksend, kt, dbuf, msg1, msg2, rgl, tbuf, tsum, hot, chg, gsend, grecv, psend, precv,
    own_sem, s_send, s_recv, k_send, k_recv, k_fwd, d_send, d_recv, m1_send, m1_recv, m2_send, m2_recv,
    t_send, t_recv, g_send, g_recv, p_send, p_recv,
):
    z, m, s = lax.axis_index("dp"), lax.axis_index("mp"), lax.axis_index("section")
    per = N // M
    T = states.shape[0]
    nl = lens_in.shape[0]
    L = T // nl
    Q = S * nl
    F, C = pol_in.shape

    def at(zz, mm, ss):
        return {"dp": zz, "mp": mm, "section": ss}

    def remote(src, dst, send, recv, to):
        return pltpu.make_async_remote_copy(
            src_ref=src, dst_ref=dst, send_sem=send, recv_sem=recv, device_id=to, device_id_type=MESH
        )

    def landed(dst, sem):
        pltpu.make_async_copy(dst, dst, sem).wait()

    plane = [
        (k, (m + k % M) % M, (s + k // M) % S) for k in range(1, S * M)
    ]
    column = [((z + dz) % N, (m + dm) % M) for dz in range(1, N) for dm in range(M)]

    def mate(k):
        if S & (S - 1):
            return (s + k) % S
        at_s, bit = s, 1
        while bit < S:
            if k & bit:
                at_s = at_s + bit - 2 * bit * ((s // bit) % 2)
            bit *= 2
        return at_s

    barrier = pltpu.get_barrier_semaphore()
    for _, mm, ss in plane:
        pl.semaphore_signal(barrier, inc=1, device_id=at(z, mm, ss), device_id_type=MESH)
    for zz, mm in column:
        pl.semaphore_signal(barrier, inc=1, device_id=at(zz, mm, s), device_id_type=MESH)

    loads = [
        pltpu.make_async_copy(src, dst, in_sem.at[n])
        for n, (src, dst) in enumerate(
            (
                (dirs_in, dirs), (pol_in, pol), (ref_in, ref), (head_in, head),
                (lens_in, lens), (gids_in, gids), (routes_in, routes), (old_in, old),
            )
        )
    ]
    for load in loads:
        load.start()
    own_copy = pltpu.make_async_copy(states, own, own_sem)
    own_copy.start()

    def columns(ii, ss):
        return states.at[:, pl.ds(pl.multiple_of((S * ii + ss) * F, F), F)]

    for ii in range(per):
        pltpu.make_async_copy(columns(ii, s), sbuf.at[ii, s], s_recv.at[ii, s]).start()
    loads[0].wait()
    dbuf[s, m] = dirs[...].astype(F32).T.astype(BF16)

    pl.semaphore_wait(barrier, S * M - 1 + (N - 1) * M)

    sent = []

    def go(copy):
        copy.start()
        sent.append(copy)

    for ds in range(1, S):
        go(remote(dbuf.at[s, m], dbuf.at[s, m], d_send.at[0, ds], d_recv.at[s, m], at(z, m, mate(ds))))
    for ds in range(1, S):
        ss = mate(ds)
        for ii in range(per):
            go(remote(columns(ii, ss), sbuf.at[ii, s], s_send.at[ii, ds], s_recv.at[ii, s], at(z, m, ss)))
    for load in loads[1:3]:
        load.wait()
    ksend[0:C, :] = pol[...].astype(F32).T.astype(BF16)
    ksend[C : 2 * C, :] = ref[...].astype(F32).T.astype(BF16)
    m_k = z // per
    k_slot = kt.at[z % per, m]
    k_sem = k_recv.at[z % per, m]
    k_out = []
    for n, step in enumerate((1, -1)):
        inside = (z + step >= 0) & (z + step < N)
        copy = remote(ksend, k_slot, k_send.at[n + 1], k_sem, at((z + step + N) % N, m_k, s))
        k_out.append((inside, copy))

        @pl.when(inside)
        def _(copy=copy):
            copy.start()

    def onward(d):
        for step in (1, -1):
            i = z - step * d
            ii = (i + N) % per
            held_here = (i >= m * per) & (i < (m + 1) * per)
            to = z + step

            @pl.when(held_here & (to >= 0) & (to < N))
            def _(ii=ii, to=to):
                for mm in range(M):
                    part = kt.at[ii, mm]
                    landed(part, k_recv.at[ii, mm])
                    remote(
                        part, part, k_fwd.at[ii, mm], k_recv.at[ii, mm], at((to + N) % N, m, s)
                    ).start()

    k_near = remote(ksend, k_slot, k_send.at[0], k_sem, at(z, m_k, s))

    @pl.when(m_k != m)
    def _():
        k_near.start()

    @pl.when(m_k == m)
    def _():
        pltpu.make_async_copy(ksend, k_slot, k_sem).start()

    for load in loads[3:]:
        load.wait()
    own_copy.wait()
    scores = lax.dot_general(
        jnp.broadcast_to(head[...].reshape(1, -1), (16, head.shape[0])), own[...], LAST, preferred_element_type=F32
    )[0:1, :]
    spot = lax.broadcasted_iota(jnp.int32, (1, L), 1)
    for r in range(nl):
        mine = jnp.where(spot < lens[r], scores[:, r * L : (r + 1) * L], 0.0)
        msg1[s, m, r : r + 1, :] = jnp.broadcast_to(jnp.sum(mine, axis=1, keepdims=True), (1, 128))
        msg1[s, m, nl + r : nl + r + 1, :] = jnp.full((1, 128), lens[r].astype(F32))
        msg1[s, m, 2 * nl + r : 2 * nl + r + 1, :] = jnp.full((1, 128), gids[r].astype(F32))
    for k, mm, ss in plane:
        go(remote(msg1.at[s, m], msg1.at[s, m], m1_send.at[k], m1_recv.at[s, m], at(z, mm, ss)))

    for ds in range(S):
        ss = mate(ds)
        if ds:
            landed(dbuf.at[ss, m], d_recv.at[ss, m])
        for dm in range(1, M):
            to = at(z, (m + dm) % M, s)
            go(remote(dbuf.at[ss, m], dbuf.at[ss, m], d_send.at[dm, ds], d_recv.at[ss, m], to))

    onward(1)
    for k, mm, ss in plane:
        landed(msg1.at[ss, mm], m1_recv.at[ss, mm])
    for t in range(S):
        total = msg1[t, 0, 0:nl, :]
        for mm in range(1, M):
            total = total + msg1[t, mm, 0:nl, :]
        rgl[0, t * nl : (t + 1) * nl, :] = total
        rgl[1, t * nl : (t + 1) * nl, :] = msg1[t, 0, nl : 2 * nl, :]
        rgl[2, t * nl : (t + 1) * nl, :] = msg1[t, 0, 2 * nl : 3 * nl, :]
    reward = rgl[0] / jnp.sqrt(rgl[1])
    lane = lax.broadcasted_iota(jnp.int32, (Q, 128), 1).astype(F32)
    member = rgl[2] == lane
    held = jnp.where(member, reward, 0.0)
    msg2[z, 0:1, :] = jnp.sum(held, axis=0, keepdims=True)
    msg2[z, 1:2, :] = jnp.sum(held * held, axis=0, keepdims=True)
    msg2[z, 2:8, :] = jnp.zeros((6, 128), F32)
    for dz in range(1, N):
        go(remote(msg2.at[z], msg2.at[z], m2_send.at[dz], m2_recv.at[z], at((z + dz) % N, m, s)))

    rows = max(16, N)
    shard = lax.broadcasted_iota(jnp.int32, (rows, T), 0)
    choose = (shard == routes[...]).astype(F32)
    upto = (
        lax.broadcasted_iota(jnp.int32, (T, T), 0) <= lax.broadcasted_iota(jnp.int32, (T, T), 1)
    ).astype(F32).astype(BF16)
    ranked = jnp.dot(choose.astype(BF16), upto, preferred_element_type=F32) - 1.0
    within = jnp.sum(ranked * choose, axis=0, keepdims=True)
    slot = routes[...].astype(F32) * width + within + (z * cap).astype(F32)
    for r in range(N):
        place = lax.broadcasted_iota(jnp.int32, (width, T), 0).astype(F32) + float(r * width)
        hot[r * width : (r + 1) * width, :] = (place == slot).astype(F32).astype(BF16)

    for d in range(2, N - 1):
        onward(d)
    for dz in range(1, N):
        landed(msg2.at[(z + dz) % N], m2_recv.at[(z + dz) % N])
    sums = msg2[0]
    for zz in range(1, N):
        sums = sums + msg2[zz]
    center = sums[0:1, :] / GROUP
    spread = sums[1:2, :] / GROUP - center * center
    own_center = jnp.sum(jnp.where(member, center, 0.0), axis=1, keepdims=True)
    own_spread = jnp.sum(jnp.where(member, spread, 0.0), axis=1, keepdims=True)
    advantage = ((reward - own_center) / jnp.sqrt(own_spread + var_offset)).astype(BF16).astype(F32)
    valid = (
        lax.broadcasted_iota(jnp.int32, (Q, L), 1).astype(F32) < rgl[1][:, 0:1]
    ).astype(F32)

    k_passed = []
    for ii in range(per):
        i = m * per + ii
        k_passed.append(((i < z) & (z < N - 1)) | ((i > z) & (z > 0)))

        @pl.when(jnp.logical_not(k_passed[ii]))
        def _(ii=ii):
            for mm in range(M):
                landed(kt.at[ii, mm], k_recv.at[ii, mm])

    for ds in range(S):
        for dm in range(1, M):
            ss, mm = mate(ds), (m + dm) % M
            landed(dbuf.at[ss, mm], d_recv.at[ss, mm])

    for ds in range(S):
        t = mate(ds)
        keys = None
        for ii in range(per):
            landed(sbuf.at[ii, t], s_recv.at[ii, t])
            part = lax.dot_general(
                kt[ii].reshape(2 * M * C, F), sbuf[ii, t], LAST, preferred_element_type=F32
            )
            keys = part if keys is None else keys + part
        for which in range(2):
            term = None
            for mm in range(M):
                low = (2 * mm + which) * C
                part = jnp.sum(dbuf[t, mm].astype(F32) * keys[low : low + C, :], axis=0, keepdims=True)
                term = part if term is None else term + part
            for r in range(nl):
                n = which * nl + r
                tbuf[s, m, t, n : n + 1, :] = term[:, r * L : (r + 1) * L]
    for k, mm, ss in plane:
        go(remote(tbuf.at[s, m], tbuf.at[s, m], t_send.at[k], t_recv.at[s, m], at(z, mm, ss)))
    for k, mm, ss in plane:
        landed(tbuf.at[ss, mm], t_recv.at[ss, mm])
    for t in range(S):
        terms = None
        for ss in range(S):
            for mm in range(M):
                terms = tbuf[ss, mm, t] if terms is None else terms + tbuf[ss, mm, t]
        tp, tr = terms[0:nl, :], terms[nl : 2 * nl, :]
        tsum[t] = tp
        adv = advantage[t * nl : (t + 1) * nl, :]
        coef = valid[t * nl : (t + 1) * nl, :] * (
            -adv * jnp.exp(tp) + kl_weight * (1.0 - jnp.exp(tr - tp))
        )
        for r in range(nl):
            q = t * nl + r
            for mm in range(M):
                chg[mm * C : (mm + 1) * C, q * L : (q + 1) * L] = (
                    dbuf[t, mm, :, r * L : (r + 1) * L].astype(F32) * coef[r : r + 1, :]
                ).astype(BF16)
    g_near = []
    for ii in range(per):
        part = jnp.dot(chg[...], sbuf[ii].reshape(S * T, F), preferred_element_type=F32)
        for mm in range(M):
            gsend[ii, mm] = part[mm * C : (mm + 1) * C, :].astype(BF16)
        zz = m * per + ii
        for dm in range(1, M):
            mm = (m + dm) % M
            go(remote(gsend.at[ii, mm], grecv.at[z], g_send.at[ii, dm], g_recv.at[z], at(zz, mm, s)))
        far = remote(gsend.at[ii, m], grecv.at[z], g_send.at[ii, 0], g_recv.at[z], at(zz, m, s))
        g_near.append((zz, far))

        @pl.when(zz != z)
        def _(far=far):
            far.start()

        @pl.when(zz == z)
        def _(ii=ii):
            pltpu.make_async_copy(gsend.at[ii, m], grecv.at[z], g_recv.at[z]).start()

        if ii == 0:
            logp = tsum[s]
            row = jnp.concatenate([logp[r : r + 1, :] for r in range(nl)], axis=1) + old[...].reshape(1, T).astype(F32)
            high = row.astype(BF16).astype(F32)
            mid = (row - high).astype(BF16).astype(F32)
            low = row - high - mid
            split = jnp.concatenate([high, mid, low, jnp.zeros((13, T), F32)], axis=0).astype(BF16)
            placed = lax.dot_general(split, hot[...], LAST, preferred_element_type=F32)
            line = placed[0:1, :] + placed[1:2, :] + placed[2:3, :]
            for r in range(N):
                psend[r] = line[:, r * width : (r + 1) * width]
            for dz in range(1, N):
                zz = (z + dz) % N
                go(remote(psend.at[zz], precv.at[z], p_send.at[dz], p_recv.at[z], at(zz, m, s)))

    precv[z] = psend[z]
    for dz in range(1, N):
        landed(precv.at[(z + dz) % N], p_recv.at[(z + dz) % N])
    packed = precv[0]
    for zz in range(1, N):
        packed = packed + precv[zz]
    pack[0] = packed[:, : N * cap]

    total = None
    for zz in range(N):
        landed(grecv.at[zz], g_recv.at[zz])
        part = grecv[zz].astype(F32)
        total = part if total is None else total + part
    grad[...] = total.T

    for copy in sent:
        copy.wait_send()

    @pl.when(m_k != m)
    def _():
        k_near.wait_send()

    for inside, copy in k_out:

        @pl.when(inside)
        def _(copy=copy):
            copy.wait_send()

    for ii in range(per):

        @pl.when(k_passed[ii])
        def _(ii=ii):
            for mm in range(M):
                part = kt.at[ii, mm]
                remote(part, part, k_fwd.at[ii, mm], k_recv.at[ii, mm], at(z, m, s)).wait_send()

    for zz, far in g_near:

        @pl.when(zz != z)
        def _(far=far):
            far.wait_send()


def body(states, direction, old_logp, lengths, group_ids, routes, reward_head, policy_k, reference_k):
    N, M, S = lax.axis_size("dp"), lax.axis_size("mp"), lax.axis_size("section")
    T = states.shape[0]
    nl = lengths.shape[0]
    L = T // nl
    F, C = policy_k.shape
    per = N // M
    Q = S * nl
    cap = max(2, 5 * T // (4 * N))
    width = -(-N * cap // 128) * 128
    vm = pl.BlockSpec(memory_space=pltpu.VMEM)
    dma = pltpu.SemaphoreType.DMA
    high = -(-3 * nl // 8) * 8
    grad_k, packed = pl.pallas_call(
        functools.partial(kernel, N, M, S, cap, width),
        out_shape=(
            jax.ShapeDtypeStruct((F, C), F32),
            jax.ShapeDtypeStruct((1, 1, N * cap), F32),
        ),
        in_specs=[pl.BlockSpec(memory_space=pltpu.HBM)] * 9,
        out_specs=(vm, vm),
        scratch_shapes=[
            pltpu.VMEM(direction.shape, BF16),
            pltpu.VMEM((T,), BF16),
            pltpu.SMEM((nl,), jnp.int32),
            pltpu.SMEM((nl,), jnp.int32),
            pltpu.VMEM((1, T), jnp.int32),
            pltpu.VMEM(reward_head.shape, BF16),
            pltpu.VMEM((F, C), BF16),
            pltpu.VMEM((F, C), BF16),
            dma((8,)),
            pltpu.VMEM(states.shape, BF16),
            pltpu.VMEM((per, S, T, F), BF16),
            pltpu.VMEM((2 * C, F), BF16),
            pltpu.VMEM((per, M, 2 * C, F), BF16),
            pltpu.VMEM((S, M, C, T), BF16),
            pltpu.VMEM((S, M, high, 128), F32),
            pltpu.VMEM((N, 8, 128), F32),
            pltpu.VMEM((3, Q, 128), F32),
            pltpu.VMEM((S, M, S, 2 * nl, L), F32),
            pltpu.VMEM((S, nl, L), F32),
            pltpu.VMEM((N * width, T), BF16),
            pltpu.VMEM((M * C, S * T), BF16),
            pltpu.VMEM((per, M, C, F), BF16),
            pltpu.VMEM((N, C, F), BF16),
            pltpu.VMEM((N, 1, width), F32),
            pltpu.VMEM((N, 1, width), F32),
            dma,
            dma((per, S)), dma((per, S)),
            dma((3,)), dma((per, M)), dma((per, M)),
            dma((M, S)), dma((S, M)),
            dma((S * M,)), dma((S, M)),
            dma((N,)), dma((N,)),
            dma((S * M,)), dma((S, M)),
            dma((per, M)), dma((N,)),
            dma((N,)), dma((N,)),
        ],
        compiler_params=pltpu.CompilerParams(
            collective_id=0, has_side_effects=True, vmem_limit_bytes=40 * 1024 * 1024
        ),
    )(*(
        pltpu.with_memory_space_constraint(operand, pltpu.HBM)
        for operand in (
            states, direction, old_logp, lengths, group_ids, routes.reshape(1, T), reward_head, policy_k, reference_k
        )
    ))
    return grad_k, packed


def solution(mesh):
    both = ("dp", "section")
    return jax.shard_map(
        body,
        mesh=mesh,
        in_specs=(
            P(both, "mp"),
            P(both, "mp"),
            P(both),
            P(both),
            P(both),
            P(both, None),
            P("mp"),
            P(both, "mp"),
            P(both, "mp"),
        ),
        out_specs=(P(both, "mp"), P("dp", "section", None)),
        check_vma=False,
    )
```

```python
import functools

import jax
import jax.numpy as jnp
from jax import lax
from jax.experimental import pallas as pl
from jax.experimental.pallas import tpu as pltpu
from jax.sharding import PartitionSpec as P

GROUP = 8
kl_weight = 0.4
var_offset = 0.25
F32 = jnp.float32
BF16 = jnp.bfloat16
MESH = pl.DeviceIdType.MESH
LAST = (((1,), (1,)), ((), ()))


def kernel(
    N, M, S, cap, width,
    states, dirs_in, old_in, lens_in, gids_in, routes_in, head_in, pol_in, ref_in,
    grad, pack,
    dirs, old, lens, gids, routes, head, pol, ref, in_sem,
    own, sbuf, ksend, kt, dbuf, msg1, msg2, rgl, tbuf, tsum, hot, chg, gsend, gkeep, crecv, grecv, psend, precv,
    own_sem, s_send, s_recv, k_send, k_recv, k_fwd, d_send, d_recv, m1_send, m1_recv, m2_send, m2_recv,
    t_send, t_recv, c_send, c_recv, g_send, g_recv, gate, p_send, p_recv,
):
    z, m, s = lax.axis_index("dp"), lax.axis_index("mp"), lax.axis_index("section")
    per = N // M
    T = states.shape[0]
    nl = lens_in.shape[0]
    L = T // nl
    Q = S * nl
    F, C = pol_in.shape

    def at(zz, mm, ss):
        return {"dp": zz, "mp": mm, "section": ss}

    def remote(src, dst, send, recv, to):
        return pltpu.make_async_remote_copy(
            src_ref=src, dst_ref=dst, send_sem=send, recv_sem=recv, device_id=to, device_id_type=MESH
        )

    def landed(dst, sem):
        pltpu.make_async_copy(dst, dst, sem).wait()

    plane = [
        (k, (m + k % M) % M, (s + k // M) % S) for k in range(1, S * M)
    ]
    column = [((z + dz) % N, (m + dm) % M) for dz in range(1, N) for dm in range(M)]

    def mate(k):
        if S & (S - 1):
            return (s + k) % S
        at_s, bit = s, 1
        while bit < S:
            if k & bit:
                at_s = at_s + bit - 2 * bit * ((s // bit) % 2)
            bit *= 2
        return at_s

    barrier = pltpu.get_barrier_semaphore()
    for _, mm, ss in plane:
        pl.semaphore_signal(barrier, inc=1, device_id=at(z, mm, ss), device_id_type=MESH)
    for zz, mm in column:
        pl.semaphore_signal(barrier, inc=1, device_id=at(zz, mm, s), device_id_type=MESH)

    loads = [
        pltpu.make_async_copy(src, dst, in_sem.at[n])
        for n, (src, dst) in enumerate(
            (
                (dirs_in, dirs), (pol_in, pol), (ref_in, ref), (head_in, head),
                (lens_in, lens), (gids_in, gids), (routes_in, routes), (old_in, old),
            )
        )
    ]
    for load in loads:
        load.start()
    own_copy = pltpu.make_async_copy(states, own, own_sem)
    own_copy.start()

    def columns(ii, ss):
        return states.at[:, pl.ds(pl.multiple_of((S * ii + ss) * F, F), F)]

    for ii in range(per):
        for h in range(2):
            rows = pl.ds(h * (T // 2), T // 2)
            pltpu.make_async_copy(
                columns(ii, s).at[rows], sbuf.at[ii, s, rows], s_recv.at[h, ii, s]
            ).start()
    for load in loads[0:3]:
        load.wait()
    ksend[0:C, :] = pol[...].astype(F32).T.astype(BF16)
    ksend[C : 2 * C, :] = ref[...].astype(F32).T.astype(BF16)
    dbuf[s, m] = dirs[...].astype(F32).T.astype(BF16)

    pl.semaphore_wait(barrier, S * M - 1 + (N - 1) * M)

    sent = []

    def go(copy):
        copy.start()
        sent.append(copy)

    for ds in range(1, S):
        go(remote(dbuf.at[s, m], dbuf.at[s, m], d_send.at[0, ds], d_recv.at[s, m], at(z, m, mate(ds))))
    m_k = z // per
    k_slot = kt.at[z % per, m]
    k_sem = k_recv.at[z % per, m]
    k_out = []

    def send_keys(h, step):
        inside = (z + step >= 0) & (z + step < N)
        half = pl.ds(h * C, C)
        sem = k_send.at[len(k_out)]
        copy = remote(ksend.at[half], k_slot.at[half], sem, k_sem, at((z + step + N) % N, m_k, s))
        k_out.append((inside, copy))

        @pl.when(inside)
        def _():
            copy.start()

    turn = m % 2
    mates = [mate(ds) for ds in range(1, S)]
    if S > 2:
        first, second = mates[0], mates[1]
        mates[0] = first + turn * (second - first)
        mates[1] = second + turn * (first - second)
    for h in range(2):
        rows = pl.ds(h * (T // 2), T // 2)
        for ii in range(per):
            if ii < 2:
                send_keys(h, 1 - 2 * ii)
            for n, ss in enumerate(mates):
                go(
                    remote(
                        columns(ii, ss).at[rows],
                        sbuf.at[ii, s, rows],
                        s_send.at[h, ii, n],
                        s_recv.at[h, ii, s],
                        at(z, m, ss),
                    )
                )

    def onward(d):
        for step in (1, -1):
            i = z - step * d
            ii = (i + N) % per
            held_here = (i >= m * per) & (i < (m + 1) * per)
            to = z + step

            @pl.when(held_here & (to >= 0) & (to < N))
            def _(ii=ii, to=to):
                for mm in range(M):
                    part = kt.at[ii, mm]
                    landed(part, k_recv.at[ii, mm])
                    remote(
                        part, part, k_fwd.at[ii, mm], k_recv.at[ii, mm], at((to + N) % N, m, s)
                    ).start()

    k_near = remote(ksend, k_slot, k_send.at[4], k_sem, at(z, m_k, s))

    @pl.when(m_k != m)
    def _():
        k_near.start()

    @pl.when(m_k == m)
    def _():
        pltpu.make_async_copy(ksend, k_slot, k_sem).start()

    for load in loads[3:]:
        load.wait()
    own_copy.wait()
    scores = lax.dot_general(
        jnp.broadcast_to(head[...].reshape(1, -1), (16, head.shape[0])), own[...], LAST, preferred_element_type=F32
    )[0:1, :]
    spot = lax.broadcasted_iota(jnp.int32, (1, L), 1)
    for r in range(nl):
        mine = jnp.where(spot < lens[r], scores[:, r * L : (r + 1) * L], 0.0)
        msg1[s, m, r : r + 1, :] = jnp.broadcast_to(jnp.sum(mine, axis=1, keepdims=True), (1, 128))
        msg1[s, m, nl + r : nl + r + 1, :] = jnp.full((1, 128), lens[r].astype(F32))
        msg1[s, m, 2 * nl + r : 2 * nl + r + 1, :] = jnp.full((1, 128), gids[r].astype(F32))
    for k, mm, ss in plane:
        go(remote(msg1.at[s, m], msg1.at[s, m], m1_send.at[k], m1_recv.at[s, m], at(z, mm, ss)))

    for ds in range(S):
        ss = mate(ds)
        if ds:
            landed(dbuf.at[ss, m], d_recv.at[ss, m])
        for dm in range(1, M):
            to = at(z, (m + dm) % M, s)
            go(remote(dbuf.at[ss, m], dbuf.at[ss, m], d_send.at[dm, ds], d_recv.at[ss, m], to))

    onward(1)
    for k, mm, ss in plane:
        landed(msg1.at[ss, mm], m1_recv.at[ss, mm])
    for t in range(S):
        total = msg1[t, 0, 0:nl, :]
        for mm in range(1, M):
            total = total + msg1[t, mm, 0:nl, :]
        rgl[0, t * nl : (t + 1) * nl, :] = total
        rgl[1, t * nl : (t + 1) * nl, :] = msg1[t, 0, nl : 2 * nl, :]
        rgl[2, t * nl : (t + 1) * nl, :] = msg1[t, 0, 2 * nl : 3 * nl, :]
    reward = rgl[0] / jnp.sqrt(rgl[1])
    lane = lax.broadcasted_iota(jnp.int32, (Q, 128), 1).astype(F32)
    member = rgl[2] == lane
    held = jnp.where(member, reward, 0.0)
    msg2[z, 0:1, :] = jnp.sum(held, axis=0, keepdims=True)
    msg2[z, 1:2, :] = jnp.sum(held * held, axis=0, keepdims=True)
    msg2[z, 2:8, :] = jnp.zeros((6, 128), F32)
    for dz in range(1, N):
        go(remote(msg2.at[z], msg2.at[z], m2_send.at[dz], m2_recv.at[z], at((z + dz) % N, m, s)))

    rows = max(16, N)
    shard = lax.broadcasted_iota(jnp.int32, (rows, T), 0)
    choose = (shard == routes[...]).astype(F32)
    upto = (
        lax.broadcasted_iota(jnp.int32, (T, T), 0) <= lax.broadcasted_iota(jnp.int32, (T, T), 1)
    ).astype(F32).astype(BF16)
    ranked = jnp.dot(choose.astype(BF16), upto, preferred_element_type=F32) - 1.0
    within = jnp.sum(ranked * choose, axis=0, keepdims=True)
    slot = routes[...].astype(F32) * width + within + (z * cap).astype(F32)
    for r in range(N):
        place = lax.broadcasted_iota(jnp.int32, (width, T), 0).astype(F32) + float(r * width)
        hot[r * width : (r + 1) * width, :] = (place == slot).astype(F32).astype(BF16)

    for d in range(2, N - 1):
        onward(d)
    for dz in range(1, N):
        landed(msg2.at[(z + dz) % N], m2_recv.at[(z + dz) % N])
    sums = msg2[0]
    for zz in range(1, N):
        sums = sums + msg2[zz]
    center = sums[0:1, :] / GROUP
    spread = sums[1:2, :] / GROUP - center * center
    own_center = jnp.sum(jnp.where(member, center, 0.0), axis=1, keepdims=True)
    own_spread = jnp.sum(jnp.where(member, spread, 0.0), axis=1, keepdims=True)
    advantage = ((reward - own_center) / jnp.sqrt(own_spread + var_offset)).astype(BF16).astype(F32)
    valid = (
        lax.broadcasted_iota(jnp.int32, (Q, L), 1).astype(F32) < rgl[1][:, 0:1]
    ).astype(F32)

    k_passed = []
    for ii in range(per):
        i = m * per + ii
        k_passed.append(((i < z) & (z < N - 1)) | ((i > z) & (z > 0)))

        @pl.when(jnp.logical_not(k_passed[ii]))
        def _(ii=ii):
            for mm in range(M):
                landed(kt.at[ii, mm], k_recv.at[ii, mm])

    for ds in range(S):
        for dm in range(1, M):
            ss, mm = mate(ds), (m + dm) % M
            landed(dbuf.at[ss, mm], d_recv.at[ss, mm])

    for ds in range(S):
        t = mate(ds)
        keys = None
        for ii in range(per):
            for h in range(2):
                landed(sbuf.at[ii, t, pl.ds(h * (T // 2), T // 2)], s_recv.at[h, ii, t])
            part = lax.dot_general(
                kt[ii].reshape(2 * M * C, F), sbuf[ii, t], LAST, preferred_element_type=F32
            )
            keys = part if keys is None else keys + part
        for which in range(2):
            term = None
            for mm in range(M):
                low = (2 * mm + which) * C
                part = jnp.sum(dbuf[t, mm].astype(F32) * keys[low : low + C, :], axis=0, keepdims=True)
                term = part if term is None else term + part
            for r in range(nl):
                n = which * nl + r
                tbuf[s, m, t, n : n + 1, :] = term[:, r * L : (r + 1) * L]
    for k, mm, ss in plane:
        go(remote(tbuf.at[s, m], tbuf.at[s, m], t_send.at[k], t_recv.at[s, m], at(z, mm, ss)))
    for k, mm, ss in plane:
        landed(tbuf.at[ss, mm], t_recv.at[ss, mm])
    for t in range(S):
        terms = None
        for ss in range(S):
            for mm in range(M):
                terms = tbuf[ss, mm, t] if terms is None else terms + tbuf[ss, mm, t]
        tp, tr = terms[0:nl, :], terms[nl : 2 * nl, :]
        tsum[t] = tp
        adv = advantage[t * nl : (t + 1) * nl, :]
        coef = valid[t * nl : (t + 1) * nl, :] * (
            -adv * jnp.exp(tp) + kl_weight * (1.0 - jnp.exp(tr - tp))
        )
        for r in range(nl):
            q = t * nl + r
            for mm in range(M):
                chg[mm * C : (mm + 1) * C, q * L : (q + 1) * L] = (
                    dbuf[t, mm, :, r * L : (r + 1) * L].astype(F32) * coef[r : r + 1, :]
                ).astype(BF16)
    pair, odd = z // 2, z % 2
    partner = z + 1 - 2 * odd
    far = m != pair
    near = m == pair
    part = jnp.dot(chg[...], sbuf[1 - odd].reshape(S * T, F), preferred_element_type=F32)
    for mm in range(M):
        gsend[0, mm] = part[mm * C : (mm + 1) * C, :].astype(BF16)

    def to_partner(mm):
        return remote(gsend.at[0, mm], crecv.at[mm], c_send.at[mm], c_recv.at[mm], at(partner, m, s))

    def to_owner(mm):
        return remote(gsend.at[1, mm], grecv.at[pair], g_send.at[mm], g_recv.at[pair], at(2 * m + odd, mm, s))

    def to_mate(mm):
        return remote(gsend.at[0, mm], grecv.at[N // 2], c_send.at[mm], g_recv.at[N // 2], at(partner, mm, s))

    def to_core(dm):
        mm = (m + dm) % M
        return remote(gsend.at[1, mm], grecv.at[pair], g_send.at[dm], g_recv.at[pair], at(z, mm, s))

    @pl.when(far)
    def _():
        for mm in range(M):
            to_partner(mm).start()

    part = jnp.dot(chg[...], sbuf[odd].reshape(S * T, F), preferred_element_type=F32)
    for mm in range(M):
        gkeep[mm] = part[mm * C : (mm + 1) * C, :]
        gsend[1, mm] = part[mm * C : (mm + 1) * C, :].astype(BF16)

    @pl.when(near)
    def _():
        for dm in range(1, M):
            to_core(dm).start()
        pltpu.make_async_copy(gsend.at[1, m], grecv.at[pair], g_recv.at[pair]).start()

    logp = tsum[s]
    row = jnp.concatenate([logp[r : r + 1, :] for r in range(nl)], axis=1) + old[...].reshape(1, T).astype(F32)
    high = row.astype(BF16).astype(F32)
    mid = (row - high).astype(BF16).astype(F32)
    low = row - high - mid
    split = jnp.concatenate([high, mid, low, jnp.zeros((13, T), F32)], axis=0).astype(BF16)
    placed = lax.dot_general(split, hot[...], LAST, preferred_element_type=F32)
    line = placed[0:1, :] + placed[1:2, :] + placed[2:3, :]
    for r in range(N):
        psend[r] = line[:, r * width : (r + 1) * width]
    for dz in range(1, N):
        zz = (z + dz) % N
        go(remote(psend.at[zz], precv.at[z], p_send.at[dz], p_recv.at[z], at(zz, m, s)))


    @pl.when(far)
    def _():
        for mm in range(M):
            landed(crecv.at[mm], c_recv.at[mm])
            gsend[1, mm] = (gkeep[mm] + crecv[mm].astype(F32)).astype(BF16)
            to_owner(mm).start()
        pl.semaphore_signal(gate, inc=1, device_id=at(z, pair, s), device_id_type=MESH)

    @pl.when(near)
    def _():
        pl.semaphore_wait(gate, M - 1)
        for mm in range(M):
            to_mate(mm).start()

    precv[z] = psend[z]
    for dz in range(1, N):
        landed(precv.at[(z + dz) % N], p_recv.at[(z + dz) % N])
    packed = precv[0]
    for zz in range(1, N):
        packed = packed + precv[zz]
    pack[0] = packed[:, : N * cap]

    total = None
    for zz in range(N // 2 + 1):
        landed(grecv.at[zz], g_recv.at[zz])
        part = grecv[zz].astype(F32)
        total = part if total is None else total + part
    grad[...] = total.T

    for copy in sent:
        copy.wait_send()

    @pl.when(m_k != m)
    def _():
        k_near.wait_send()

    for inside, copy in k_out:

        @pl.when(inside)
        def _(copy=copy):
            copy.wait_send()

    for ii in range(per):

        @pl.when(k_passed[ii])
        def _(ii=ii):
            for mm in range(M):
                part = kt.at[ii, mm]
                remote(part, part, k_fwd.at[ii, mm], k_recv.at[ii, mm], at(z, m, s)).wait_send()

    @pl.when(far)
    def _():
        for mm in range(M):
            to_partner(mm).wait_send()
            to_owner(mm).wait_send()

    @pl.when(near)
    def _():
        for mm in range(M):
            to_mate(mm).wait_send()
        for dm in range(1, M):
            to_core(dm).wait_send()


def body(states, direction, old_logp, lengths, group_ids, routes, reward_head, policy_k, reference_k):
    N, M, S = lax.axis_size("dp"), lax.axis_size("mp"), lax.axis_size("section")
    T = states.shape[0]
    nl = lengths.shape[0]
    L = T // nl
    F, C = policy_k.shape
    per = N // M
    Q = S * nl
    cap = max(2, 5 * T // (4 * N))
    width = -(-N * cap // 128) * 128
    vm = pl.BlockSpec(memory_space=pltpu.VMEM)
    dma = pltpu.SemaphoreType.DMA
    high = -(-3 * nl // 8) * 8
    grad_k, packed = pl.pallas_call(
        functools.partial(kernel, N, M, S, cap, width),
        out_shape=(
            jax.ShapeDtypeStruct((F, C), F32),
            jax.ShapeDtypeStruct((1, 1, N * cap), F32),
        ),
        in_specs=[pl.BlockSpec(memory_space=pltpu.HBM)] * 9,
        out_specs=(vm, vm),
        scratch_shapes=[
            pltpu.VMEM(direction.shape, BF16),
            pltpu.VMEM((T,), BF16),
            pltpu.SMEM((nl,), jnp.int32),
            pltpu.SMEM((nl,), jnp.int32),
            pltpu.VMEM((1, T), jnp.int32),
            pltpu.VMEM(reward_head.shape, BF16),
            pltpu.VMEM((F, C), BF16),
            pltpu.VMEM((F, C), BF16),
            dma((8,)),
            pltpu.VMEM(states.shape, BF16),
            pltpu.VMEM((per, S, T, F), BF16),
            pltpu.VMEM((2 * C, F), BF16),
            pltpu.VMEM((per, M, 2 * C, F), BF16),
            pltpu.VMEM((S, M, C, T), BF16),
            pltpu.VMEM((S, M, high, 128), F32),
            pltpu.VMEM((N, 8, 128), F32),
            pltpu.VMEM((3, Q, 128), F32),
            pltpu.VMEM((S, M, S, 2 * nl, L), F32),
            pltpu.VMEM((S, nl, L), F32),
            pltpu.VMEM((N * width, T), BF16),
            pltpu.VMEM((M * C, S * T), BF16),
            pltpu.VMEM((per, M, C, F), BF16),
            pltpu.VMEM((M, C, F), F32),
            pltpu.VMEM((M, C, F), BF16),
            pltpu.VMEM((N // 2 + 1, C, F), BF16),
            pltpu.VMEM((N, 1, width), F32),
            pltpu.VMEM((N, 1, width), F32),
            dma,
            dma((2, per, S)), dma((2, per, S)),
            dma((5,)), dma((per, M)), dma((per, M)),
            dma((M, S)), dma((S, M)),
            dma((S * M,)), dma((S, M)),
            dma((N,)), dma((N,)),
            dma((S * M,)), dma((S, M)),
            dma((M,)), dma((M,)),
            dma((M,)), dma((N // 2 + 1,)),
            pltpu.SemaphoreType.REGULAR,
            dma((N,)), dma((N,)),
        ],
        compiler_params=pltpu.CompilerParams(
            collective_id=0, has_side_effects=True, vmem_limit_bytes=40 * 1024 * 1024
        ),
    )(*(
        pltpu.with_memory_space_constraint(operand, pltpu.HBM)
        for operand in (
            states, direction, old_logp, lengths, group_ids, routes.reshape(1, T), reward_head, policy_k, reference_k
        )
    ))
    return grad_k, packed


def solution(mesh):
    both = ("dp", "section")
    return jax.shard_map(
        body,
        mesh=mesh,
        in_specs=(
            P(both, "mp"),
            P(both, "mp"),
            P(both),
            P(both),
            P(both),
            P(both, None),
            P("mp"),
            P(both, "mp"),
            P(both, "mp"),
        ),
        out_specs=(P(both, "mp"), P("dp", "section", None)),
        check_vma=False,
    )
```

```python
import functools

import jax
import jax.numpy as jnp
from jax import lax
from jax.experimental import pallas as pl
from jax.experimental.pallas import tpu as pltpu
from jax.sharding import PartitionSpec as P

GROUP = 8
kl_weight = 0.4
var_offset = 0.25
F32 = jnp.float32
BF16 = jnp.bfloat16
MESH = pl.DeviceIdType.MESH
LAST = (((1,), (1,)), ((), ()))


def kernel(
    N, M, S, cap, width,
    states, dirs_in, old_in, lens_in, gids_in, routes_in, head_in, pol_in, ref_in,
    grad, pack,
    dirs, old, lens, gids, routes, head, pol, ref, in_sem,
    own, sbuf, ksend, kt, dbuf, msg1, msg2, rgl, tbuf, tsum, hot, chg, gsend, grecv, psend, precv,
    own_sem, s_send, s_recv, k_send, k_recv, d_send, d_recv, m1_send, m1_recv, m2_send, m2_recv,
    t_send, t_recv, g_send, g_recv, p_send, p_recv,
):
    z, m, s = lax.axis_index("dp"), lax.axis_index("mp"), lax.axis_index("section")
    per = N // M
    T = states.shape[0]
    nl = lens_in.shape[0]
    L = T // nl
    Q = S * nl
    F, C = pol_in.shape

    def at(zz, mm, ss):
        return {"dp": zz, "mp": mm, "section": ss}

    def remote(src, dst, send, recv, to):
        return pltpu.make_async_remote_copy(
            src_ref=src, dst_ref=dst, send_sem=send, recv_sem=recv, device_id=to, device_id_type=MESH
        )

    def landed(dst, sem):
        pltpu.make_async_copy(dst, dst, sem).wait()

    plane = [
        (k, (m + k % M) % M, (s + k // M) % S) for k in range(1, S * M)
    ]
    column = [((z + dz) % N, (m + dm) % M) for dz in range(1, N) for dm in range(M)]

    barrier = pltpu.get_barrier_semaphore()
    for _, mm, ss in plane:
        pl.semaphore_signal(barrier, inc=1, device_id=at(z, mm, ss), device_id_type=MESH)
    for zz, mm in column:
        pl.semaphore_signal(barrier, inc=1, device_id=at(zz, mm, s), device_id_type=MESH)

    loads = [
        pltpu.make_async_copy(src, dst, in_sem.at[n])
        for n, (src, dst) in enumerate(
            (
                (dirs_in, dirs), (pol_in, pol), (ref_in, ref), (head_in, head),
                (lens_in, lens), (gids_in, gids), (routes_in, routes), (old_in, old),
            )
        )
    ]
    for load in loads:
        load.start()
    own_copy = pltpu.make_async_copy(states, own, own_sem)
    own_copy.start()

    def columns(ii, ss):
        return states.at[:, pl.ds(pl.multiple_of((S * ii + ss) * F, F), F)]

    for ii in range(per):
        pltpu.make_async_copy(columns(ii, s), sbuf.at[ii, s], s_recv.at[ii, s]).start()
    loads[0].wait()
    dbuf[s, m] = dirs[...].astype(F32).T.astype(BF16)

    pl.semaphore_wait(barrier, S * M - 1 + (N - 1) * M)

    sent = []

    def go(copy):
        copy.start()
        sent.append(copy)

    for ds in range(1, S):
        ss = (s + ds) % S
        go(remote(dbuf.at[s, m], dbuf.at[s, m], d_send.at[0, ds], d_recv.at[s, m], at(z, m, ss)))
    for ii in range(per):
        for ds in range(1, S):
            ss = (s + ds) % S
            go(remote(columns(ii, ss), sbuf.at[ii, s], s_send.at[ii, ds], s_recv.at[ii, s], at(z, m, ss)))
    for load in loads[1:3]:
        load.wait()
    ksend[0:C, :] = pol[...].astype(F32).T.astype(BF16)
    ksend[C : 2 * C, :] = ref[...].astype(F32).T.astype(BF16)
    m_k = z // per
    k_slot = kt.at[z % per, m]
    k_sem = k_recv.at[z % per, m]
    for dz in range(1, N):
        go(remote(ksend, k_slot, k_send.at[dz], k_sem, at((z + dz) % N, m_k, s)))
    k_near = remote(ksend, k_slot, k_send.at[0], k_sem, at(z, m_k, s))

    @pl.when(m_k != m)
    def _():
        k_near.start()

    @pl.when(m_k == m)
    def _():
        pltpu.make_async_copy(ksend, k_slot, k_sem).start()

    for load in loads[3:]:
        load.wait()
    own_copy.wait()
    scores = lax.dot_general(
        jnp.broadcast_to(head[...].reshape(1, -1), (16, head.shape[0])), own[...], LAST, preferred_element_type=F32
    )[0:1, :]
    spot = lax.broadcasted_iota(jnp.int32, (1, L), 1)
    for r in range(nl):
        mine = jnp.where(spot < lens[r], scores[:, r * L : (r + 1) * L], 0.0)
        msg1[s, m, r : r + 1, :] = jnp.broadcast_to(jnp.sum(mine, axis=1, keepdims=True), (1, 128))
        msg1[s, m, nl + r : nl + r + 1, :] = jnp.full((1, 128), lens[r].astype(F32))
        msg1[s, m, 2 * nl + r : 2 * nl + r + 1, :] = jnp.full((1, 128), gids[r].astype(F32))
    for k, mm, ss in plane:
        go(remote(msg1.at[s, m], msg1.at[s, m], m1_send.at[k], m1_recv.at[s, m], at(z, mm, ss)))

    for ds in range(S):
        ss = (s + ds) % S
        if ds:
            landed(dbuf.at[ss, m], d_recv.at[ss, m])
        for dm in range(1, M):
            to = at(z, (m + dm) % M, s)
            go(remote(dbuf.at[ss, m], dbuf.at[ss, m], d_send.at[dm, ds], d_recv.at[ss, m], to))

    for k, mm, ss in plane:
        landed(msg1.at[ss, mm], m1_recv.at[ss, mm])
    for t in range(S):
        total = msg1[t, 0, 0:nl, :]
        for mm in range(1, M):
            total = total + msg1[t, mm, 0:nl, :]
        rgl[0, t * nl : (t + 1) * nl, :] = total
        rgl[1, t * nl : (t + 1) * nl, :] = msg1[t, 0, nl : 2 * nl, :]
        rgl[2, t * nl : (t + 1) * nl, :] = msg1[t, 0, 2 * nl : 3 * nl, :]
    reward = rgl[0] / jnp.sqrt(rgl[1])
    lane = lax.broadcasted_iota(jnp.int32, (Q, 128), 1).astype(F32)
    member = rgl[2] == lane
    held = jnp.where(member, reward, 0.0)
    msg2[z, 0:1, :] = jnp.sum(held, axis=0, keepdims=True)
    msg2[z, 1:2, :] = jnp.sum(held * held, axis=0, keepdims=True)
    msg2[z, 2:8, :] = jnp.zeros((6, 128), F32)
    for dz in range(1, N):
        go(remote(msg2.at[z], msg2.at[z], m2_send.at[dz], m2_recv.at[z], at((z + dz) % N, m, s)))
    for dz in range(1, N):
        landed(msg2.at[(z + dz) % N], m2_recv.at[(z + dz) % N])
    sums = msg2[0]
    for zz in range(1, N):
        sums = sums + msg2[zz]
    center = sums[0:1, :] / GROUP
    spread = sums[1:2, :] / GROUP - center * center
    own_center = jnp.sum(jnp.where(member, center, 0.0), axis=1, keepdims=True)
    own_spread = jnp.sum(jnp.where(member, spread, 0.0), axis=1, keepdims=True)
    advantage = ((reward - own_center) / jnp.sqrt(own_spread + var_offset)).astype(BF16).astype(F32)
    valid = (
        lax.broadcasted_iota(jnp.int32, (Q, L), 1).astype(F32) < rgl[1][:, 0:1]
    ).astype(F32)

    for ii in range(per):
        for mm in range(M):
            landed(kt.at[ii, mm], k_recv.at[ii, mm])
    for ds in range(S):
        for dm in range(1, M):
            ss, mm = (s + ds) % S, (m + dm) % M
            landed(dbuf.at[ss, mm], d_recv.at[ss, mm])

    @pl.loop(0, S)
    def _(ds):
        t = (s + ds) % S
        keys = None
        for ii in range(per):
            landed(sbuf.at[ii, t], s_recv.at[ii, t])
            part = lax.dot_general(
                kt[ii].reshape(2 * M * C, F), sbuf[ii, t], LAST, preferred_element_type=F32
            )
            keys = part if keys is None else keys + part
        for which in range(2):
            term = None
            for mm in range(M):
                low = (2 * mm + which) * C
                part = jnp.sum(dbuf[t, mm].astype(F32) * keys[low : low + C, :], axis=0, keepdims=True)
                term = part if term is None else term + part
            for r in range(nl):
                n = which * nl + r
                tbuf[s, m, t, n : n + 1, :] = term[:, r * L : (r + 1) * L]

    for k, mm, ss in plane:
        go(remote(tbuf.at[s, m], tbuf.at[s, m], t_send.at[k], t_recv.at[s, m], at(z, mm, ss)))
    for k, mm, ss in plane:
        landed(tbuf.at[ss, mm], t_recv.at[ss, mm])
    for t in range(S):
        terms = None
        for ss in range(S):
            for mm in range(M):
                terms = tbuf[ss, mm, t] if terms is None else terms + tbuf[ss, mm, t]
        tp, tr = terms[0:nl, :], terms[nl : 2 * nl, :]
        tsum[t] = tp
        adv = advantage[t * nl : (t + 1) * nl, :]
        coef = valid[t * nl : (t + 1) * nl, :] * (
            -adv * jnp.exp(tp) + kl_weight * (1.0 - jnp.exp(tr - tp))
        )
        for r in range(nl):
            q = t * nl + r
            for mm in range(M):
                chg[mm * C : (mm + 1) * C, q * L : (q + 1) * L] = (
                    dbuf[t, mm, :, r * L : (r + 1) * L].astype(F32) * coef[r : r + 1, :]
                ).astype(BF16)
    g_near = []
    for ii in range(per):
        part = jnp.dot(chg[...], sbuf[ii].reshape(S * T, F), preferred_element_type=F32)
        for mm in range(M):
            gsend[ii, mm] = part[mm * C : (mm + 1) * C, :].astype(BF16)
        zz = m * per + ii
        for dm in range(1, M):
            mm = (m + dm) % M
            go(remote(gsend.at[ii, mm], grecv.at[z], g_send.at[ii, dm], g_recv.at[z], at(zz, mm, s)))
        far = remote(gsend.at[ii, m], grecv.at[z], g_send.at[ii, 0], g_recv.at[z], at(zz, m, s))
        g_near.append((zz, far))

        @pl.when(zz != z)
        def _(far=far):
            far.start()

        @pl.when(zz == z)
        def _(ii=ii):
            pltpu.make_async_copy(gsend.at[ii, m], grecv.at[z], g_recv.at[z]).start()

    rows = max(16, N)
    shard = lax.broadcasted_iota(jnp.int32, (rows, T), 0)
    choose = (shard == routes[...]).astype(F32)
    upto = (
        lax.broadcasted_iota(jnp.int32, (T, T), 0) <= lax.broadcasted_iota(jnp.int32, (T, T), 1)
    ).astype(F32).astype(BF16)
    ranked = jnp.dot(choose.astype(BF16), upto, preferred_element_type=F32) - 1.0
    within = jnp.sum(ranked * choose, axis=0, keepdims=True)
    slot = routes[...].astype(F32) * width + within + (z * cap).astype(F32)
    for r in range(N):
        place = lax.broadcasted_iota(jnp.int32, (width, T), 0).astype(F32) + float(r * width)
        hot[r * width : (r + 1) * width, :] = (place == slot).astype(F32).astype(BF16)

    logp = tsum[s]
    row = jnp.concatenate([logp[r : r + 1, :] for r in range(nl)], axis=1) + old[...].reshape(1, T).astype(F32)
    high = row.astype(BF16).astype(F32)
    mid = (row - high).astype(BF16).astype(F32)
    low = row - high - mid
    split = jnp.concatenate([high, mid, low, jnp.zeros((13, T), F32)], axis=0).astype(BF16)
    placed = lax.dot_general(split, hot[...], LAST, preferred_element_type=F32)
    line = placed[0:1, :] + placed[1:2, :] + placed[2:3, :]
    for r in range(N):
        psend[r] = line[:, r * width : (r + 1) * width]
    for dz in range(1, N):
        zz = (z + dz) % N
        go(remote(psend.at[zz], precv.at[z], p_send.at[dz], p_recv.at[z], at(zz, m, s)))

    precv[z] = psend[z]
    for dz in range(1, N):
        landed(precv.at[(z + dz) % N], p_recv.at[(z + dz) % N])
    packed = precv[0]
    for zz in range(1, N):
        packed = packed + precv[zz]
    pack[0] = packed[:, : N * cap]

    total = None
    for zz in range(N):
        landed(grecv.at[zz], g_recv.at[zz])
        part = grecv[zz].astype(F32)
        total = part if total is None else total + part
    grad[...] = total.T

    for copy in sent:
        copy.wait_send()

    @pl.when(m_k != m)
    def _():
        k_near.wait_send()

    for zz, far in g_near:

        @pl.when(zz != z)
        def _(far=far):
            far.wait_send()


def body(states, direction, old_logp, lengths, group_ids, routes, reward_head, policy_k, reference_k):
    N, M, S = lax.axis_size("dp"), lax.axis_size("mp"), lax.axis_size("section")
    T = states.shape[0]
    nl = lengths.shape[0]
    L = T // nl
    F, C = policy_k.shape
    per = N // M
    Q = S * nl
    cap = max(2, 5 * T // (4 * N))
    width = -(-N * cap // 128) * 128
    vm = pl.BlockSpec(memory_space=pltpu.VMEM)
    dma = pltpu.SemaphoreType.DMA
    high = -(-3 * nl // 8) * 8
    grad_k, packed = pl.pallas_call(
        functools.partial(kernel, N, M, S, cap, width),
        out_shape=(
            jax.ShapeDtypeStruct((F, C), F32),
            jax.ShapeDtypeStruct((1, 1, N * cap), F32),
        ),
        in_specs=[pl.BlockSpec(memory_space=pltpu.HBM)] * 9,
        out_specs=(vm, vm),
        scratch_shapes=[
            pltpu.VMEM(direction.shape, BF16),
            pltpu.VMEM((T,), BF16),
            pltpu.SMEM((nl,), jnp.int32),
            pltpu.SMEM((nl,), jnp.int32),
            pltpu.VMEM((1, T), jnp.int32),
            pltpu.VMEM(reward_head.shape, BF16),
            pltpu.VMEM((F, C), BF16),
            pltpu.VMEM((F, C), BF16),
            dma((8,)),
            pltpu.VMEM(states.shape, BF16),
            pltpu.VMEM((per, S, T, F), BF16),
            pltpu.VMEM((2 * C, F), BF16),
            pltpu.VMEM((per, M, 2 * C, F), BF16),
            pltpu.VMEM((S, M, C, T), BF16),
            pltpu.VMEM((S, M, high, 128), F32),
            pltpu.VMEM((N, 8, 128), F32),
            pltpu.VMEM((3, Q, 128), F32),
            pltpu.VMEM((S, M, S, 2 * nl, L), F32),
            pltpu.VMEM((S, nl, L), F32),
            pltpu.VMEM((N * width, T), BF16),
            pltpu.VMEM((M * C, S * T), BF16),
            pltpu.VMEM((per, M, C, F), BF16),
            pltpu.VMEM((N, C, F), BF16),
            pltpu.VMEM((N, 1, width), F32),
            pltpu.VMEM((N, 1, width), F32),
            dma,
            dma((per, S)), dma((per, S)),
            dma((N,)), dma((per, M)),
            dma((M, S)), dma((S, M)),
            dma((S * M,)), dma((S, M)),
            dma((N,)), dma((N,)),
            dma((S * M,)), dma((S, M)),
            dma((per, M)), dma((N,)),
            dma((N,)), dma((N,)),
        ],
        compiler_params=pltpu.CompilerParams(
            collective_id=0, has_side_effects=True, vmem_limit_bytes=40 * 1024 * 1024
        ),
    )(*(
        pltpu.with_memory_space_constraint(operand, pltpu.HBM)
        for operand in (
            states, direction, old_logp, lengths, group_ids, routes.reshape(1, T), reward_head, policy_k, reference_k
        )
    ))
    return grad_k, packed


def solution(mesh):
    both = ("dp", "section")
    return jax.shard_map(
        body,
        mesh=mesh,
        in_specs=(
            P(both, "mp"),
            P(both, "mp"),
            P(both),
            P(both),
            P(both),
            P(both, None),
            P("mp"),
            P(both, "mp"),
            P(both, "mp"),
        ),
        out_specs=(P(both, "mp"), P("dp", "section", None)),
        check_vma=False,
    )
```

```python
import functools

import jax
import jax.numpy as jnp
from jax import lax
from jax.experimental import pallas as pl
from jax.experimental.pallas import tpu as pltpu
from jax.sharding import PartitionSpec as P

GROUP = 8
kl_weight = 0.4
var_offset = 0.25
F32 = jnp.float32
BF16 = jnp.bfloat16
MESH = pl.DeviceIdType.MESH
LAST = (((1,), (1,)), ((), ()))


def kernel(
    N, M, S, cap, width,
    states, dirs_in, old_in, lens_in, gids_in, routes_in, head_in, pol_in, ref_in,
    grad, pack,
    dirs, old, lens, gids, routes, head, pol, ref, in_sem,
    own, sbuf, ksend, kt, dbuf, msg1, msg2, rgl, tbuf, tsum, hot, chg, gsend, grecv, psend, precv,
    own_sem, s_send, s_recv, k_send, k_recv, d_send, d_recv, m1_send, m1_recv, m2_send, m2_recv,
    t_send, t_recv, g_send, g_recv, p_send, p_recv,
):
    z, m, s = lax.axis_index("dp"), lax.axis_index("mp"), lax.axis_index("section")
    per = N // M
    T = states.shape[0]
    nl = lens_in.shape[0]
    L = T // nl
    Q = S * nl
    F, C = pol_in.shape

    def at(zz, mm, ss):
        return {"dp": zz, "mp": mm, "section": ss}

    def remote(src, dst, send, recv, to):
        return pltpu.make_async_remote_copy(
            src_ref=src, dst_ref=dst, send_sem=send, recv_sem=recv, device_id=to, device_id_type=MESH
        )

    def landed(dst, sem):
        pltpu.make_async_copy(dst, dst, sem).wait()

    plane = [
        (k, (m + k % M) % M, (s + k // M) % S) for k in range(1, S * M)
    ]
    column = [((z + dz) % N, (m + dm) % M) for dz in range(1, N) for dm in range(M)]

    barrier = pltpu.get_barrier_semaphore()
    for _, mm, ss in plane:
        pl.semaphore_signal(barrier, inc=1, device_id=at(z, mm, ss), device_id_type=MESH)
    for zz, mm in column:
        pl.semaphore_signal(barrier, inc=1, device_id=at(zz, mm, s), device_id_type=MESH)

    loads = [
        pltpu.make_async_copy(src, dst, in_sem.at[n])
        for n, (src, dst) in enumerate(
            (
                (dirs_in, dirs), (pol_in, pol), (ref_in, ref), (head_in, head),
                (lens_in, lens), (gids_in, gids), (routes_in, routes), (old_in, old),
            )
        )
    ]
    for load in loads:
        load.start()
    own_copy = pltpu.make_async_copy(states, own, own_sem)
    own_copy.start()

    def columns(ii, ss):
        return states.at[:, pl.ds(pl.multiple_of((S * ii + ss) * F, F), F)]

    for ii in range(per):
        pltpu.make_async_copy(columns(ii, s), sbuf.at[ii, s], s_recv.at[ii, s]).start()
    for load in loads[0:3]:
        load.wait()
    ksend[0:C, :] = pol[...].astype(F32).T.astype(BF16)
    ksend[C : 2 * C, :] = ref[...].astype(F32).T.astype(BF16)
    dbuf[s, m] = dirs[...].astype(F32).T.astype(BF16)

    pl.semaphore_wait(barrier, S * M - 1 + (N - 1) * M)

    sent = []

    def go(copy):
        copy.start()
        sent.append(copy)

    for ds in range(1, S):
        ss = (s + ds) % S
        go(remote(dbuf.at[s, m], dbuf.at[s, m], d_send.at[0, ds], d_recv.at[s, m], at(z, m, ss)))
    m_k = z // per
    k_slot = kt.at[z % per, m]
    k_sem = k_recv.at[z % per, m]
    order = [(ds, ii) for ii in range(per) for ds in range(1, S)]
    for n in range(max(len(order), 3 * (N - 1))):
        if n % 3 == 0 and n // 3 < N - 1:
            dz = n // 3 + 1
            go(remote(ksend, k_slot, k_send.at[dz], k_sem, at((z + dz) % N, m_k, s)))
        if n < len(order):
            ds, ii = order[n]
            ss = (s + 1 + (ds - 1 + m % 2) % max(1, S - 1)) % S
            go(remote(columns(ii, ss), sbuf.at[ii, s], s_send.at[ii, ds], s_recv.at[ii, s], at(z, m, ss)))
    k_near = remote(ksend, k_slot, k_send.at[0], k_sem, at(z, m_k, s))

    @pl.when(m_k != m)
    def _():
        k_near.start()

    @pl.when(m_k == m)
    def _():
        pltpu.make_async_copy(ksend, k_slot, k_sem).start()

    for load in loads[3:]:
        load.wait()
    own_copy.wait()
    scores = lax.dot_general(
        jnp.broadcast_to(head[...].reshape(1, -1), (16, head.shape[0])), own[...], LAST, preferred_element_type=F32
    )[0:1, :]
    spot = lax.broadcasted_iota(jnp.int32, (1, L), 1)
    for r in range(nl):
        mine = jnp.where(spot < lens[r], scores[:, r * L : (r + 1) * L], 0.0)
        msg1[s, m, r : r + 1, :] = jnp.broadcast_to(jnp.sum(mine, axis=1, keepdims=True), (1, 128))
        msg1[s, m, nl + r : nl + r + 1, :] = jnp.full((1, 128), lens[r].astype(F32))
        msg1[s, m, 2 * nl + r : 2 * nl + r + 1, :] = jnp.full((1, 128), gids[r].astype(F32))
    for k, mm, ss in plane:
        go(remote(msg1.at[s, m], msg1.at[s, m], m1_send.at[k], m1_recv.at[s, m], at(z, mm, ss)))

    for ds in range(S):
        ss = (s + ds) % S
        if ds:
            landed(dbuf.at[ss, m], d_recv.at[ss, m])
        for dm in range(1, M):
            to = at(z, (m + dm) % M, s)
            go(remote(dbuf.at[ss, m], dbuf.at[ss, m], d_send.at[dm, ds], d_recv.at[ss, m], to))

    rows = max(16, N)
    shard = lax.broadcasted_iota(jnp.int32, (rows, T), 0)
    choose = (shard == routes[...]).astype(F32)
    upto = (
        lax.broadcasted_iota(jnp.int32, (T, T), 0) <= lax.broadcasted_iota(jnp.int32, (T, T), 1)
    ).astype(F32).astype(BF16)
    ranked = jnp.dot(choose.astype(BF16), upto, preferred_element_type=F32) - 1.0
    within = jnp.sum(ranked * choose, axis=0, keepdims=True)
    slot = routes[...].astype(F32) * width + within + (z * cap).astype(F32)
    for r in range(N):
        place = lax.broadcasted_iota(jnp.int32, (width, T), 0).astype(F32) + float(r * width)
        hot[r * width : (r + 1) * width, :] = (place == slot).astype(F32).astype(BF16)

    for k, mm, ss in plane:
        landed(msg1.at[ss, mm], m1_recv.at[ss, mm])
    for t in range(S):
        total = msg1[t, 0, 0:nl, :]
        for mm in range(1, M):
            total = total + msg1[t, mm, 0:nl, :]
        rgl[0, t * nl : (t + 1) * nl, :] = total
        rgl[1, t * nl : (t + 1) * nl, :] = msg1[t, 0, nl : 2 * nl, :]
        rgl[2, t * nl : (t + 1) * nl, :] = msg1[t, 0, 2 * nl : 3 * nl, :]
    reward = rgl[0] / jnp.sqrt(rgl[1])
    lane = lax.broadcasted_iota(jnp.int32, (Q, 128), 1).astype(F32)
    member = rgl[2] == lane
    held = jnp.where(member, reward, 0.0)
    msg2[z, 0:1, :] = jnp.sum(held, axis=0, keepdims=True)
    msg2[z, 1:2, :] = jnp.sum(held * held, axis=0, keepdims=True)
    msg2[z, 2:8, :] = jnp.zeros((6, 128), F32)
    for dz in range(1, N):
        go(remote(msg2.at[z], msg2.at[z], m2_send.at[dz], m2_recv.at[z], at((z + dz) % N, m, s)))
    for dz in range(1, N):
        landed(msg2.at[(z + dz) % N], m2_recv.at[(z + dz) % N])
    sums = msg2[0]
    for zz in range(1, N):
        sums = sums + msg2[zz]
    center = sums[0:1, :] / GROUP
    spread = sums[1:2, :] / GROUP - center * center
    own_center = jnp.sum(jnp.where(member, center, 0.0), axis=1, keepdims=True)
    own_spread = jnp.sum(jnp.where(member, spread, 0.0), axis=1, keepdims=True)
    advantage = ((reward - own_center) / jnp.sqrt(own_spread + var_offset)).astype(BF16).astype(F32)
    valid = (
        lax.broadcasted_iota(jnp.int32, (Q, L), 1).astype(F32) < rgl[1][:, 0:1]
    ).astype(F32)

    for ii in range(per):
        for mm in range(M):
            landed(kt.at[ii, mm], k_recv.at[ii, mm])
    for ds in range(S):
        for dm in range(1, M):
            ss, mm = (s + ds) % S, (m + dm) % M
            landed(dbuf.at[ss, mm], d_recv.at[ss, mm])

    @pl.loop(0, S)
    def _(ds):
        t = (s + ds) % S
        keys = None
        for ii in range(per):
            landed(sbuf.at[ii, t], s_recv.at[ii, t])
            part = lax.dot_general(
                kt[ii].reshape(2 * M * C, F), sbuf[ii, t], LAST, preferred_element_type=F32
            )
            keys = part if keys is None else keys + part
        for which in range(2):
            term = None
            for mm in range(M):
                low = (2 * mm + which) * C
                part = jnp.sum(dbuf[t, mm].astype(F32) * keys[low : low + C, :], axis=0, keepdims=True)
                term = part if term is None else term + part
            for r in range(nl):
                n = which * nl + r
                tbuf[s, m, t, n : n + 1, :] = term[:, r * L : (r + 1) * L]

    for k, mm, ss in plane:
        go(remote(tbuf.at[s, m], tbuf.at[s, m], t_send.at[k], t_recv.at[s, m], at(z, mm, ss)))
    for k, mm, ss in plane:
        landed(tbuf.at[ss, mm], t_recv.at[ss, mm])
    for t in range(S):
        terms = None
        for ss in range(S):
            for mm in range(M):
                terms = tbuf[ss, mm, t] if terms is None else terms + tbuf[ss, mm, t]
        tsum[t] = terms
    logp = tsum[s]
    row = jnp.concatenate([logp[r : r + 1, :] for r in range(nl)], axis=1) + old[...].reshape(1, T).astype(F32)
    high = row.astype(BF16).astype(F32)
    mid = (row - high).astype(BF16).astype(F32)
    low = row - high - mid
    split = jnp.concatenate([high, mid, low, jnp.zeros((13, T), F32)], axis=0).astype(BF16)
    placed = lax.dot_general(split, hot[...], LAST, preferred_element_type=F32)
    line = placed[0:1, :] + placed[1:2, :] + placed[2:3, :]
    for r in range(N):
        psend[r] = line[:, r * width : (r + 1) * width]
    for dz in range(1, N):
        zz = (z + dz) % N
        go(remote(psend.at[zz], precv.at[z], p_send.at[dz], p_recv.at[z], at(zz, m, s)))

    for t in range(S):
        tp, tr = tsum[t, 0:nl, :], tsum[t, nl : 2 * nl, :]
        adv = advantage[t * nl : (t + 1) * nl, :]
        coef = valid[t * nl : (t + 1) * nl, :] * (
            -adv * jnp.exp(tp) + kl_weight * (1.0 - jnp.exp(tr - tp))
        )
        for r in range(nl):
            q = t * nl + r
            for mm in range(M):
                chg[mm * C : (mm + 1) * C, q * L : (q + 1) * L] = (
                    dbuf[t, mm, :, r * L : (r + 1) * L].astype(F32) * coef[r : r + 1, :]
                ).astype(BF16)
    g_near = []
    above = (m > z // per).astype(jnp.int32)
    for n in range(per):
        ii = n + above * (per - 1 - 2 * n)
        part = jnp.dot(chg[...], sbuf[ii].reshape(S * T, F), preferred_element_type=F32)
        for mm in range(M):
            gsend[ii, mm] = part[mm * C : (mm + 1) * C, :].astype(BF16)
        zz = m * per + ii
        for dm in range(1, M):
            mm = (m + dm) % M
            go(remote(gsend.at[ii, mm], grecv.at[z], g_send.at[ii, dm], g_recv.at[z], at(zz, mm, s)))
        far = remote(gsend.at[ii, m], grecv.at[z], g_send.at[ii, 0], g_recv.at[z], at(zz, m, s))
        g_near.append((zz, far))

        @pl.when(zz != z)
        def _(far=far):
            far.start()

        @pl.when(zz == z)
        def _(ii=ii):
            pltpu.make_async_copy(gsend.at[ii, m], grecv.at[z], g_recv.at[z]).start()

    precv[z] = psend[z]
    for dz in range(1, N):
        landed(precv.at[(z + dz) % N], p_recv.at[(z + dz) % N])
    packed = precv[0]
    for zz in range(1, N):
        packed = packed + precv[zz]
    pack[0] = packed[:, : N * cap]

    total = None
    for zz in range(N):
        landed(grecv.at[zz], g_recv.at[zz])
        part = grecv[zz].astype(F32)
        total = part if total is None else total + part
    grad[...] = total.T

    for copy in sent:
        copy.wait_send()

    @pl.when(m_k != m)
    def _():
        k_near.wait_send()

    for zz, far in g_near:

        @pl.when(zz != z)
        def _(far=far):
            far.wait_send()


def body(states, direction, old_logp, lengths, group_ids, routes, reward_head, policy_k, reference_k):
    N, M, S = lax.axis_size("dp"), lax.axis_size("mp"), lax.axis_size("section")
    T = states.shape[0]
    nl = lengths.shape[0]
    L = T // nl
    F, C = policy_k.shape
    per = N // M
    Q = S * nl
    cap = max(2, 5 * T // (4 * N))
    width = -(-N * cap // 128) * 128
    vm = pl.BlockSpec(memory_space=pltpu.VMEM)
    dma = pltpu.SemaphoreType.DMA
    high = -(-3 * nl // 8) * 8
    grad_k, packed = pl.pallas_call(
        functools.partial(kernel, N, M, S, cap, width),
        out_shape=(
            jax.ShapeDtypeStruct((F, C), F32),
            jax.ShapeDtypeStruct((1, 1, N * cap), F32),
        ),
        in_specs=[pl.BlockSpec(memory_space=pltpu.HBM)] * 9,
        out_specs=(vm, vm),
        scratch_shapes=[
            pltpu.VMEM(direction.shape, BF16),
            pltpu.VMEM((T,), BF16),
            pltpu.SMEM((nl,), jnp.int32),
            pltpu.SMEM((nl,), jnp.int32),
            pltpu.VMEM((1, T), jnp.int32),
            pltpu.VMEM(reward_head.shape, BF16),
            pltpu.VMEM((F, C), BF16),
            pltpu.VMEM((F, C), BF16),
            dma((8,)),
            pltpu.VMEM(states.shape, BF16),
            pltpu.VMEM((per, S, T, F), BF16),
            pltpu.VMEM((2 * C, F), BF16),
            pltpu.VMEM((per, M, 2 * C, F), BF16),
            pltpu.VMEM((S, M, C, T), BF16),
            pltpu.VMEM((S, M, high, 128), F32),
            pltpu.VMEM((N, 8, 128), F32),
            pltpu.VMEM((3, Q, 128), F32),
            pltpu.VMEM((S, M, S, 2 * nl, L), F32),
            pltpu.VMEM((S, 2 * nl, L), F32),
            pltpu.VMEM((N * width, T), BF16),
            pltpu.VMEM((M * C, S * T), BF16),
            pltpu.VMEM((per, M, C, F), BF16),
            pltpu.VMEM((N, C, F), BF16),
            pltpu.VMEM((N, 1, width), F32),
            pltpu.VMEM((N, 1, width), F32),
            dma,
            dma((per, S)), dma((per, S)),
            dma((N,)), dma((per, M)),
            dma((M, S)), dma((S, M)),
            dma((S * M,)), dma((S, M)),
            dma((N,)), dma((N,)),
            dma((S * M,)), dma((S, M)),
            dma((per, M)), dma((N,)),
            dma((N,)), dma((N,)),
        ],
        compiler_params=pltpu.CompilerParams(
            collective_id=0, has_side_effects=True, vmem_limit_bytes=40 * 1024 * 1024
        ),
    )(*(
        pltpu.with_memory_space_constraint(operand, pltpu.HBM)
        for operand in (
            states, direction, old_logp, lengths, group_ids, routes.reshape(1, T), reward_head, policy_k, reference_k
        )
    ))
    return grad_k, packed


def solution(mesh):
    both = ("dp", "section")
    return jax.shard_map(
        body,
        mesh=mesh,
        in_specs=(
            P(both, "mp"),
            P(both, "mp"),
            P(both),
            P(both),
            P(both),
            P(both, None),
            P("mp"),
            P(both, "mp"),
            P(both, "mp"),
        ),
        out_specs=(P(both, "mp"), P("dp", "section", None)),
        check_vma=False,
    )
```

```python
import functools

import jax
import jax.numpy as jnp
from jax import lax
from jax.experimental import pallas as pl
from jax.experimental.pallas import tpu as pltpu
from jax.sharding import PartitionSpec as P

GROUP = 8
kl_weight = 0.4
var_offset = 0.25
F32 = jnp.float32
BF16 = jnp.bfloat16
MESH = pl.DeviceIdType.MESH
LAST = (((1,), (1,)), ((), ()))


def kernel(
    N, M, S, cap, width,
    states, dirs_in, old_in, lens_in, gids_in, routes_in, head_in, pol_in, ref_in,
    grad, pack,
    dirs, old, lens, gids, routes, head, pol, ref, in_sem,
    own, sbuf, ksend, kt, dbuf, msg1, msg2, rgl, tbuf, tsum, hot, chg, gsend, grecv, psend, precv,
    own_sem, s_send, s_recv, k_send, k_recv, d_send, d_recv, m1_send, m1_recv, m2_send, m2_recv,
    t_send, t_recv, g_send, g_recv, p_send, p_recv,
):
    z, m, s = lax.axis_index("dp"), lax.axis_index("mp"), lax.axis_index("section")
    per = N // M
    T = states.shape[0]
    nl = lens_in.shape[0]
    L = T // nl
    Q = S * nl
    F, C = pol_in.shape

    def at(zz, mm, ss):
        return {"dp": zz, "mp": mm, "section": ss}

    def remote(src, dst, send, recv, to):
        return pltpu.make_async_remote_copy(
            src_ref=src, dst_ref=dst, send_sem=send, recv_sem=recv, device_id=to, device_id_type=MESH
        )

    def landed(dst, sem):
        pltpu.make_async_copy(dst, dst, sem).wait()

    plane = [
        (k, (m + k % M) % M, (s + k // M) % S) for k in range(1, S * M)
    ]
    column = [((z + dz) % N, (m + dm) % M) for dz in range(1, N) for dm in range(M)]

    barrier = pltpu.get_barrier_semaphore()
    for _, mm, ss in plane:
        pl.semaphore_signal(barrier, inc=1, device_id=at(z, mm, ss), device_id_type=MESH)
    for zz, mm in column:
        pl.semaphore_signal(barrier, inc=1, device_id=at(zz, mm, s), device_id_type=MESH)

    loads = [
        pltpu.make_async_copy(src, dst, in_sem.at[n])
        for n, (src, dst) in enumerate(
            (
                (dirs_in, dirs), (pol_in, pol), (ref_in, ref), (head_in, head),
                (lens_in, lens), (gids_in, gids), (routes_in, routes), (old_in, old),
            )
        )
    ]
    for load in loads:
        load.start()
    own_copy = pltpu.make_async_copy(states, own, own_sem)
    own_copy.start()

    def columns(ii, ss):
        return states.at[:, pl.ds(pl.multiple_of((S * ii + ss) * F, F), F)]

    for ii in range(per):
        pltpu.make_async_copy(columns(ii, s), sbuf.at[ii, s], s_recv.at[ii, s]).start()
    loads[0].wait()
    dbuf[s, m] = dirs[...].astype(F32).T.astype(BF16)

    pl.semaphore_wait(barrier, S * M - 1 + (N - 1) * M)

    sent = []

    def go(copy):
        copy.start()
        sent.append(copy)

    for ds in range(1, S):
        ss = (s + ds) % S
        go(remote(dbuf.at[s, m], dbuf.at[s, m], d_send.at[0, ds], d_recv.at[s, m], at(z, m, ss)))
    m_k = z // per
    k_slot = kt.at[z % per, m]
    k_sem = k_recv.at[z % per, m]
    order = [(ds, ii) for ii in range(per) for ds in range(1, S)]
    for n in range(max(len(order), S - 1 + N - 1)):
        if n == S - 1:
            for load in loads[1:3]:
                load.wait()
            ksend[0:C, :] = pol[...].astype(F32).T.astype(BF16)
            ksend[C : 2 * C, :] = ref[...].astype(F32).T.astype(BF16)
        if n >= S - 1 and n - (S - 1) < N - 1:
            dz = n - (S - 1) + 1
            go(remote(ksend, k_slot, k_send.at[dz], k_sem, at((z + dz) % N, m_k, s)))
        if n < len(order):
            ds, ii = order[n]
            ss = (s + 1 + (ds - 1 + m % 2) % max(1, S - 1)) % S
            go(remote(columns(ii, ss), sbuf.at[ii, s], s_send.at[ii, ds], s_recv.at[ii, s], at(z, m, ss)))
    k_near = remote(ksend, k_slot, k_send.at[0], k_sem, at(z, m_k, s))

    @pl.when(m_k != m)
    def _():
        k_near.start()

    @pl.when(m_k == m)
    def _():
        pltpu.make_async_copy(ksend, k_slot, k_sem).start()

    for load in loads[3:]:
        load.wait()
    own_copy.wait()
    scores = lax.dot_general(
        jnp.broadcast_to(head[...].reshape(1, -1), (16, head.shape[0])), own[...], LAST, preferred_element_type=F32
    )[0:1, :]
    spot = lax.broadcasted_iota(jnp.int32, (1, L), 1)
    for r in range(nl):
        mine = jnp.where(spot < lens[r], scores[:, r * L : (r + 1) * L], 0.0)
        msg1[s, m, r : r + 1, :] = jnp.broadcast_to(jnp.sum(mine, axis=1, keepdims=True), (1, 128))
        msg1[s, m, nl + r : nl + r + 1, :] = jnp.full((1, 128), lens[r].astype(F32))
        msg1[s, m, 2 * nl + r : 2 * nl + r + 1, :] = jnp.full((1, 128), gids[r].astype(F32))
    for k, mm, ss in plane:
        go(remote(msg1.at[s, m], msg1.at[s, m], m1_send.at[k], m1_recv.at[s, m], at(z, mm, ss)))

    for ds in range(S):
        ss = (s + ds) % S
        if ds:
            landed(dbuf.at[ss, m], d_recv.at[ss, m])
        for dm in range(1, M):
            to = at(z, (m + dm) % M, s)
            go(remote(dbuf.at[ss, m], dbuf.at[ss, m], d_send.at[dm, ds], d_recv.at[ss, m], to))

    rows = max(16, N)
    shard = lax.broadcasted_iota(jnp.int32, (rows, T), 0)
    choose = (shard == routes[...]).astype(F32)
    upto = (
        lax.broadcasted_iota(jnp.int32, (T, T), 0) <= lax.broadcasted_iota(jnp.int32, (T, T), 1)
    ).astype(F32).astype(BF16)
    ranked = jnp.dot(choose.astype(BF16), upto, preferred_element_type=F32) - 1.0
    within = jnp.sum(ranked * choose, axis=0, keepdims=True)
    slot = routes[...].astype(F32) * width + within + (z * cap).astype(F32)
    for r in range(N):
        place = lax.broadcasted_iota(jnp.int32, (width, T), 0).astype(F32) + float(r * width)
        hot[r * width : (r + 1) * width, :] = (place == slot).astype(F32).astype(BF16)

    for k, mm, ss in plane:
        landed(msg1.at[ss, mm], m1_recv.at[ss, mm])
    for t in range(S):
        total = msg1[t, 0, 0:nl, :]
        for mm in range(1, M):
            total = total + msg1[t, mm, 0:nl, :]
        rgl[0, t * nl : (t + 1) * nl, :] = total
        rgl[1, t * nl : (t + 1) * nl, :] = msg1[t, 0, nl : 2 * nl, :]
        rgl[2, t * nl : (t + 1) * nl, :] = msg1[t, 0, 2 * nl : 3 * nl, :]
    reward = rgl[0] / jnp.sqrt(rgl[1])
    lane = lax.broadcasted_iota(jnp.int32, (Q, 128), 1).astype(F32)
    member = rgl[2] == lane
    held = jnp.where(member, reward, 0.0)
    msg2[z, 0:1, :] = jnp.sum(held, axis=0, keepdims=True)
    msg2[z, 1:2, :] = jnp.sum(held * held, axis=0, keepdims=True)
    msg2[z, 2:8, :] = jnp.zeros((6, 128), F32)
    for dz in range(1, N):
        go(remote(msg2.at[z], msg2.at[z], m2_send.at[dz], m2_recv.at[z], at((z + dz) % N, m, s)))
    for dz in range(1, N):
        landed(msg2.at[(z + dz) % N], m2_recv.at[(z + dz) % N])
    sums = msg2[0]
    for zz in range(1, N):
        sums = sums + msg2[zz]
    center = sums[0:1, :] / GROUP
    spread = sums[1:2, :] / GROUP - center * center
    own_center = jnp.sum(jnp.where(member, center, 0.0), axis=1, keepdims=True)
    own_spread = jnp.sum(jnp.where(member, spread, 0.0), axis=1, keepdims=True)
    advantage = ((reward - own_center) / jnp.sqrt(own_spread + var_offset)).astype(BF16).astype(F32)
    valid = (
        lax.broadcasted_iota(jnp.int32, (Q, L), 1).astype(F32) < rgl[1][:, 0:1]
    ).astype(F32)

    for ii in range(per):
        for mm in range(M):
            landed(kt.at[ii, mm], k_recv.at[ii, mm])
    for ds in range(S):
        for dm in range(1, M):
            ss, mm = (s + ds) % S, (m + dm) % M
            landed(dbuf.at[ss, mm], d_recv.at[ss, mm])

    @pl.loop(0, S)
    def _(ds):
        near_by = 1 + (ds + S - 2 + m % 2) % max(1, S - 1)
        t = (s + S - near_by * ((ds + S - 1) // S)) % S
        keys = None
        for ii in range(per):
            landed(sbuf.at[ii, t], s_recv.at[ii, t])
            part = lax.dot_general(
                kt[ii].reshape(2 * M * C, F), sbuf[ii, t], LAST, preferred_element_type=F32
            )
            keys = part if keys is None else keys + part
        for which in range(2):
            term = None
            for mm in range(M):
                low = (2 * mm + which) * C
                part = jnp.sum(dbuf[t, mm].astype(F32) * keys[low : low + C, :], axis=0, keepdims=True)
                term = part if term is None else term + part
            for r in range(nl):
                n = which * nl + r
                tbuf[s, m, t, n : n + 1, :] = term[:, r * L : (r + 1) * L]

    for k, mm, ss in plane:
        go(remote(tbuf.at[s, m], tbuf.at[s, m], t_send.at[k], t_recv.at[s, m], at(z, mm, ss)))
    for k, mm, ss in plane:
        landed(tbuf.at[ss, mm], t_recv.at[ss, mm])
    for t in range(S):
        terms = None
        for ss in range(S):
            for mm in range(M):
                terms = tbuf[ss, mm, t] if terms is None else terms + tbuf[ss, mm, t]
        tsum[t] = terms
    logp = tsum[s]
    row = jnp.concatenate([logp[r : r + 1, :] for r in range(nl)], axis=1) + old[...].reshape(1, T).astype(F32)
    high = row.astype(BF16).astype(F32)
    mid = (row - high).astype(BF16).astype(F32)
    low = row - high - mid
    split = jnp.concatenate([high, mid, low, jnp.zeros((13, T), F32)], axis=0).astype(BF16)
    placed = lax.dot_general(split, hot[...], LAST, preferred_element_type=F32)
    line = placed[0:1, :] + placed[1:2, :] + placed[2:3, :]
    for r in range(N):
        psend[r] = line[:, r * width : (r + 1) * width]
    for dz in range(1, N):
        zz = (z + dz) % N
        go(remote(psend.at[zz], precv.at[z], p_send.at[dz], p_recv.at[z], at(zz, m, s)))

    for t in range(S):
        tp, tr = tsum[t, 0:nl, :], tsum[t, nl : 2 * nl, :]
        adv = advantage[t * nl : (t + 1) * nl, :]
        coef = valid[t * nl : (t + 1) * nl, :] * (
            -adv * jnp.exp(tp) + kl_weight * (1.0 - jnp.exp(tr - tp))
        )
        for r in range(nl):
            q = t * nl + r
            for mm in range(M):
                chg[mm * C : (mm + 1) * C, q * L : (q + 1) * L] = (
                    dbuf[t, mm, :, r * L : (r + 1) * L].astype(F32) * coef[r : r + 1, :]
                ).astype(BF16)
    g_near = []
    above = (m > z // per).astype(jnp.int32)
    for n in range(per):
        ii = n + above * (per - 1 - 2 * n)
        part = jnp.dot(chg[...], sbuf[ii].reshape(S * T, F), preferred_element_type=F32)
        for mm in range(M):
            gsend[ii, mm] = part[mm * C : (mm + 1) * C, :].astype(BF16)
        zz = m * per + ii
        for dm in range(1, M):
            mm = (m + dm) % M
            go(remote(gsend.at[ii, mm], grecv.at[z], g_send.at[ii, dm], g_recv.at[z], at(zz, mm, s)))
        far = remote(gsend.at[ii, m], grecv.at[z], g_send.at[ii, 0], g_recv.at[z], at(zz, m, s))
        g_near.append((zz, far))

        @pl.when(zz != z)
        def _(far=far):
            far.start()

        @pl.when(zz == z)
        def _(ii=ii):
            pltpu.make_async_copy(gsend.at[ii, m], grecv.at[z], g_recv.at[z]).start()

    precv[z] = psend[z]
    for dz in range(1, N):
        landed(precv.at[(z + dz) % N], p_recv.at[(z + dz) % N])
    packed = precv[0]
    for zz in range(1, N):
        packed = packed + precv[zz]
    pack[0] = packed[:, : N * cap]

    total = None
    for zz in range(N):
        landed(grecv.at[zz], g_recv.at[zz])
        part = grecv[zz].astype(F32)
        total = part if total is None else total + part
    grad[...] = total.T

    for copy in sent:
        copy.wait_send()

    @pl.when(m_k != m)
    def _():
        k_near.wait_send()

    for zz, far in g_near:

        @pl.when(zz != z)
        def _(far=far):
            far.wait_send()


def body(states, direction, old_logp, lengths, group_ids, routes, reward_head, policy_k, reference_k):
    N, M, S = lax.axis_size("dp"), lax.axis_size("mp"), lax.axis_size("section")
    T = states.shape[0]
    nl = lengths.shape[0]
    L = T // nl
    F, C = policy_k.shape
    per = N // M
    Q = S * nl
    cap = max(2, 5 * T // (4 * N))
    width = -(-N * cap // 128) * 128
    vm = pl.BlockSpec(memory_space=pltpu.VMEM)
    dma = pltpu.SemaphoreType.DMA
    high = -(-3 * nl // 8) * 8
    grad_k, packed = pl.pallas_call(
        functools.partial(kernel, N, M, S, cap, width),
        out_shape=(
            jax.ShapeDtypeStruct((F, C), F32),
            jax.ShapeDtypeStruct((1, 1, N * cap), F32),
        ),
        in_specs=[pl.BlockSpec(memory_space=pltpu.HBM)] * 9,
        out_specs=(vm, vm),
        scratch_shapes=[
            pltpu.VMEM(direction.shape, BF16),
            pltpu.VMEM((T,), BF16),
            pltpu.SMEM((nl,), jnp.int32),
            pltpu.SMEM((nl,), jnp.int32),
            pltpu.VMEM((1, T), jnp.int32),
            pltpu.VMEM(reward_head.shape, BF16),
            pltpu.VMEM((F, C), BF16),
            pltpu.VMEM((F, C), BF16),
            dma((8,)),
            pltpu.VMEM(states.shape, BF16),
            pltpu.VMEM((per, S, T, F), BF16),
            pltpu.VMEM((2 * C, F), BF16),
            pltpu.VMEM((per, M, 2 * C, F), BF16),
            pltpu.VMEM((S, M, C, T), BF16),
            pltpu.VMEM((S, M, high, 128), F32),
            pltpu.VMEM((N, 8, 128), F32),
            pltpu.VMEM((3, Q, 128), F32),
            pltpu.VMEM((S, M, S, 2 * nl, L), F32),
            pltpu.VMEM((S, 2 * nl, L), F32),
            pltpu.VMEM((N * width, T), BF16),
            pltpu.VMEM((M * C, S * T), BF16),
            pltpu.VMEM((per, M, C, F), BF16),
            pltpu.VMEM((N, C, F), BF16),
            pltpu.VMEM((N, 1, width), F32),
            pltpu.VMEM((N, 1, width), F32),
            dma,
            dma((per, S)), dma((per, S)),
            dma((N,)), dma((per, M)),
            dma((M, S)), dma((S, M)),
            dma((S * M,)), dma((S, M)),
            dma((N,)), dma((N,)),
            dma((S * M,)), dma((S, M)),
            dma((per, M)), dma((N,)),
            dma((N,)), dma((N,)),
        ],
        compiler_params=pltpu.CompilerParams(
            collective_id=0, has_side_effects=True, vmem_limit_bytes=40 * 1024 * 1024
        ),
    )(*(
        pltpu.with_memory_space_constraint(operand, pltpu.HBM)
        for operand in (
            states, direction, old_logp, lengths, group_ids, routes.reshape(1, T), reward_head, policy_k, reference_k
        )
    ))
    return grad_k, packed


def solution(mesh):
    both = ("dp", "section")
    return jax.shard_map(
        body,
        mesh=mesh,
        in_specs=(
            P(both, "mp"),
            P(both, "mp"),
            P(both),
            P(both),
            P(both),
            P(both, None),
            P("mp"),
            P(both, "mp"),
            P(both, "mp"),
        ),
        out_specs=(P(both, "mp"), P("dp", "section", None)),
        check_vma=False,
    )
```
